32 devices in a mesh: row: 8 (over z, y), col: 4 (over x, core).
Axes of the slice: x: 2, y: 2, z: 4, core: 2. Of those that a mesh axis runs over, the one named last changes fastest.
Arguments:
- factor: float32 [1024, 1024], P('row', 'col'), may hold values from -0.375 to 0.375
- rhs: float32 [1024, 512], P('row', 'col'), may hold values from -6 to 6
- parent: int32 [7], replicated, may hold values from 4 to 6, as said below
- bounds: int32 [8], replicated, may hold values from 0 to 8, as said below
- slot: int32 [8], replicated, may hold values from 0 to 7, each once
- structure: int32 [7, 8], replicated, may hold values 0 or 1
Outputs:
- solution: float32 [1024, 512], P('row', 'col')
The draws below stay inside these ranges and needn't reach their ends.
Inputs may be any that keep to these rules, and one draw needn't show every extreme that they name: parent[s] is 4 or 5 for s = 0 to 3, and 6 for s = 4, 5, 6 (the root is its own entry). bounds[0] = 0, bounds[7] = 8, strictly increasing; supernode s holds logical blocks bounds[s] to bounds[s+1] - 1. `slot`: a permutation.
All inputs are finite; a program needn't handle non-finite values.
Results may differ from the reference program's by a relative error of at most 0.0001.
Values sent between devices are 32-bit elements; how exact they have to be, the bound alone decides.
No kernel may reach another device: no remote copies, remote signals or barrier semaphores. Data moves between devices by JAX's collectives and lax.ppermute only.
A program may use at most 64 MiB of HBM per device.

```python
import jax
import jax.numpy as jnp
from jax import lax

B = 128
NRHS = 512
NODES = 7
NBLK = 8


def draw_parent(key, part):
    leaves = jax.random.randint(key, (4,), 4, 6).astype(jnp.int32)
    return jnp.concatenate([leaves, jnp.full((3,), 6, jnp.int32)])


def draw_bounds(key, part):
    least = NBLK // 8
    spare = NBLK - 7 * least
    picks = jnp.sort(jax.random.permutation(key, spare + 6)[:6].astype(jnp.int32))
    steps_in = jnp.arange(1, 7, dtype=jnp.int32)
    cuts = steps_in * least + picks - (steps_in - 1)
    return jnp.concatenate([jnp.zeros((1,), jnp.int32), cuts.astype(jnp.int32), jnp.full((1,), NBLK, jnp.int32)])


def plant(entries, own_key, low, top_value):
    shape = entries.shape
    spot = [jax.random.randint(jax.random.fold_in(own_key, axis), (), 0, shape[axis]) for axis in range(len(shape))]
    entries = entries.at[tuple(spot)].set(low)
    longest = shape.index(max(shape))
    spot[longest] = (spot[longest] + 1) % shape[longest]
    return entries.at[tuple(spot)].set(top_value)


def level_of(key, shape, shards, smallest, top_value):
    def one(dim, parts):
        draws = jax.random.uniform(jax.random.fold_in(jax.random.fold_in(key, 6), dim), (parts,), jnp.float32, smallest / len(shards), top_value / len(shards))
        return jnp.repeat(jnp.exp(draws), shape[dim] // parts).reshape((-1,) + (1,) * (len(shape) - dim - 1))

    factor_of = one(*shards[0])
    for cut in shards[1:]:
        factor_of = factor_of * one(*cut)
    return factor_of


def centred(stream_key, dims, deviation, bound, shards=(), held_as=jnp.bfloat16):
    result = deviation * jax.random.normal(stream_key, dims, jnp.float32)
    if shards:
        result = result * level_of(stream_key, dims, shards, -0.22, 0.18)
    return jnp.clip(result, -bound, bound).astype(held_as)


def setup_inputs(seed: int = 0) -> dict:
    key_list = jax.random.split(jax.random.key(seed), 7)
    factor = centred(key_list[0], (NBLK * B, NBLK * B), (B * NBLK // 4) ** -0.5, 0.375, ((0, 8), (1, 4)), jnp.float32)
    rhs = centred(key_list[1], (NBLK * B, NRHS), 1.0, 6.0, ((0, 8), (1, 4)), jnp.float32)
    parent = draw_parent(jax.random.fold_in(key_list[6], 71), 0)
    bounds = draw_bounds(jax.random.fold_in(key_list[6], 71), 0)
    slot = jax.random.permutation(key_list[4], NBLK).astype(jnp.int32)
    structure = plant((jax.random.randint(key_list[5], (NODES, NBLK), 0, 4) < 3).astype(jnp.int32), jax.random.fold_in(key_list[5], 1), 0, 1)
    return {"factor": factor, "rhs": rhs, "parent": parent, "bounds": bounds, "slot": slot, "structure": structure}


def block_masks(parent, bounds, slot, structure):
    count = slot.shape[0]
    ar = jnp.arange(count, dtype=jnp.int32)
    logical = jnp.sum(jnp.where(slot[:, None] == ar[None, :], ar[:, None], 0), axis=0).astype(jnp.int32)
    node = jnp.sum((logical[:, None] >= bounds[None, 1:7]).astype(jnp.int32), axis=1).astype(jnp.int32)
    level = (node >= 4).astype(jnp.int32) + (node >= 6).astype(jnp.int32)
    nodes = jnp.arange(7, dtype=jnp.int32)
    grand = parent[parent]
    ancestor = ((nodes[None, :] == parent[:, None]) | (nodes[None, :] == grand[:, None])) & (nodes[None, :] != nodes[:, None])
    same = node[:, None] == node[None, :]
    listed = structure[node[None, :], logical[:, None]] == 1
    link = ancestor[node[None, :], node[:, None]] & listed
    return level, same, link


def expand(matrix, mask, bsz):
    count = mask.shape[0]
    shaped = matrix.reshape(count, bsz, count, bsz) * mask[:, None, :, None].astype(jnp.float32)
    return shaped.reshape(matrix.shape)


def reference(factor, rhs, parent, bounds, slot, structure):
    count = slot.shape[0]
    bsz = factor.shape[0] // count
    level, same, link = block_masks(parent, bounds, slot, structure)
    diag_part = expand(factor, same, bsz)
    link_part = expand(factor, link, bsz)
    acc = jnp.zeros(rhs.shape, jnp.float32)
    solution = jnp.zeros(rhs.shape, jnp.float32)
    for section in range(3):
        rows = jnp.repeat(level == section, bsz)[:, None]
        solved = jnp.where(rows, jnp.dot(diag_part, rhs - acc, precision=lax.Precision.HIGHEST, preferred_element_type=jnp.float32), 0.0)
        solution = solution + solved
        if section < 2:
            acc = acc + jnp.dot(link_part, solved, precision=lax.Precision.HIGHEST, preferred_element_type=jnp.float32)
    return solution
```

```python
import functools

import jax
import jax.numpy as jnp
from jax import lax
from jax.experimental import pallas as pl
from jax.experimental.pallas import tpu as pltpu
from jax.sharding import PartitionSpec as P

SMEM = pl.BlockSpec(memory_space=pltpu.SMEM)
VMEM = pl.BlockSpec(memory_space=pltpu.VMEM)
HIGHEST = lax.Precision.HIGHEST


def block_masks(parent, bounds, slot, structure):
    count = slot.shape[0]
    ar = jnp.arange(count, dtype=jnp.int32)
    logical = jnp.sum(jnp.where(slot[:, None] == ar[None, :], ar[:, None], 0), axis=0)
    node = jnp.sum((logical[:, None] >= bounds[None, 1:7]).astype(jnp.int32), axis=1)
    level = (node >= 4).astype(jnp.int32) + (node >= 6).astype(jnp.int32)
    nodes = jnp.arange(7, dtype=jnp.int32)
    grand = parent[parent]
    ancestor = ((nodes[None, :] == parent[:, None]) | (nodes[None, :] == grand[:, None])) & (
        nodes[None, :] != nodes[:, None]
    )
    node_hot = (node[:, None] == nodes[None, :]).astype(jnp.float32)
    perm_hot = (logical[:, None] == ar[None, :]).astype(jnp.float32)
    listed_store = jnp.dot(structure.astype(jnp.float32), perm_hot.T, precision=HIGHEST)
    anc_pairs = jnp.dot(
        node_hot, jnp.dot(ancestor.astype(jnp.float32), node_hot.T, precision=HIGHEST), precision=HIGHEST
    )
    list_pairs = jnp.dot(node_hot, listed_store, precision=HIGHEST)
    link = (anc_pairs * list_pairs).T > 0.5
    same = node[:, None] == node[None, :]
    return level, same, link


def masked(block_rows, mask):
    rblocks, width = mask.shape
    bsz = block_rows.shape[0] // rblocks
    shaped = block_rows.reshape(rblocks, bsz, width, bsz) * mask[:, None, :, None].astype(jnp.float32)
    return shaped.reshape(block_rows.shape)


def general_body(factor, rhs, parent, bounds, slot, structure, n_row):
    level, same, link = block_masks(parent, bounds, slot, structure)
    held = slot.shape[0] // n_row
    bsz = factor.shape[0] // held
    first = lax.axis_index("row") * held
    level_mine = lax.dynamic_slice_in_dim(level, first, held, 0)
    same_mine = lax.dynamic_slice_in_dim(same, first, held, 0)
    link_mine = lax.dynamic_slice_in_dim(link, first, held, 0)
    full_rows = lax.all_gather(factor, "col", axis=1, tiled=True)
    diag_part = masked(full_rows, same_mine)
    link_part = masked(full_rows, link_mine)

    def product(matrix, vector):
        return jnp.dot(
            matrix,
            lax.all_gather(vector, "row", axis=0, tiled=True),
            precision=HIGHEST,
            preferred_element_type=jnp.float32,
        )

    acc = jnp.zeros(rhs.shape, jnp.float32)
    result = jnp.zeros(rhs.shape, jnp.float32)
    for section in range(3):
        rows = jnp.repeat(level_mine == section, bsz)[:, None]
        solved = jnp.where(rows, product(diag_part, rhs - acc), 0.0)
        result = result + solved
        if section < 2:
            acc = acc + product(link_part, solved)
    return result


MASK = 0
SAME = 1
LEVEL = 2
LINK = 4
FACTS = 32


def facts_kernel(parent, bounds, slot, structure, factor, rhs, facts, packed, logical):
    width = factor.shape[1]
    packed[:, :width] = factor[...]
    packed[:, width:] = rhs[...]
    p = lax.axis_index("row")
    c = lax.axis_index("col")
    for i in range(8):
        logical[slot[i]] = i
    wide = jnp.int32(0)
    for s in range(1, 7):
        wide = wide + (bounds[s] == s).astype(jnp.int32)
    m = slot[wide] ^ slot[wide + 1]
    facts[MASK] = m

    def node_of(q):
        at = logical[q]
        total = jnp.int32(0)
        for s in range(1, 7):
            total = total + (at >= bounds[s]).astype(jnp.int32)
        return total

    nodes = [node_of(p), node_of(p ^ m)]
    places = [logical[p], logical[p ^ m]]
    facts[SAME] = (nodes[0] == nodes[1]).astype(jnp.int32)
    for r in range(2):
        facts[LEVEL + r] = (nodes[r] >= 4).astype(jnp.int32) + (nodes[r] >= 6).astype(jnp.int32)
    for k in range(8):
        below = node_of(k ^ (2 * c))
        up = parent[below]
        top = parent[up]
        for r in range(2):
            above = ((nodes[r] == up) | (nodes[r] == top)) & (nodes[r] != below)
            listed = structure[below, places[r]] == 1
            facts[LINK + 8 * r + k] = (above & listed).astype(jnp.int32)


def take_diagonal(p, c, m, rows, diag, bsz):
    for r in range(2):
        for s in range(2):
            place = (p ^ (2 * c)) if s == 0 else (p ^ m ^ (2 * c))
            for k in range(8):

                @pl.when(place == k)
                def _(r=r, s=s, k=k):
                    at = (k % 2) * bsz
                    diag[r, s] = rows[r][k // 2][:, at : at + bsz]


def dot(a, b):
    return jnp.dot(a, b, precision=HIGHEST, preferred_element_type=jnp.float32)


def solve_pair(facts, diag, section, mine, pair):
    same = facts[SAME].astype(jnp.float32)
    on = [(facts[LEVEL + r] == section).astype(jnp.float32) for r in range(2)]
    y_mine = (dot(diag[0, 0], mine) + same * dot(diag[0, 1], pair)) * on[0]
    y_pair = (dot(diag[1, 1], pair) + same * dot(diag[1, 0], mine)) * on[1]
    return y_mine, y_pair


def first_kernel(facts, rhs, f0, f1, f2, f3, g0, g1, g2, g3, y, diag):
    bsz = rhs.shape[0]
    p = lax.axis_index("row")
    c = lax.axis_index("col")
    take_diagonal(p, c, facts[MASK], [[f0, f1, f2, f3], [g0, g1, g2, g3]], diag, bsz)
    y_mine, y_pair = solve_pair(facts, diag, 0, rhs[...], g0[:, 2 * bsz :])
    y[:bsz] = y_mine
    y[bsz:] = y_pair


def update(facts, rows, ys, picks, y_all, link, bsz):
    p = lax.axis_index("row")
    c = lax.axis_index("col")
    m = facts[MASK]
    for y, pick in zip(ys, picks):
        for s in range(2):
            place = p ^ pick ^ (2 * c) ^ (m if s else 0)
            y_all[pl.ds(pl.multiple_of(place * bsz, bsz), bsz), :] = y[s * bsz : (s + 1) * bsz, :]
    for r in range(2):
        for k in range(8):
            at = (k % 2) * bsz
            on = facts[LINK + 8 * r + k].astype(jnp.float32)
            link[r * bsz : (r + 1) * bsz, k * bsz : (k + 1) * bsz] = rows[r][k // 2][:, at : at + bsz] * on
    return dot(link[...], y_all[...])


def coset_picks(m):
    first = jnp.where(m == 1, 2, 1)
    second = jnp.where(m >= 4, 2, 4)
    return [0, first, second, first ^ second]


def second_kernel(facts, rhs, f0, f1, f2, f3, g0, g1, g2, g3, y, ya, yb, yc, y1, t, diag, y_all, link):
    bsz = rhs.shape[0]
    p = lax.axis_index("row")
    c = lax.axis_index("col")
    rows = [[f0, f1, f2, f3], [g0, g1, g2, g3]]
    take_diagonal(p, c, facts[MASK], rows, diag, bsz)
    acc = update(facts, rows, [y, ya, yb, yc], coset_picks(facts[MASK]), y_all, link, bsz)
    mine = rhs[...] - acc[:bsz]
    pair = g0[:, 2 * bsz :] - acc[bsz:]
    t[:bsz] = mine
    t[bsz:] = pair
    y_mine, y_pair = solve_pair(facts, diag, 1, mine, pair)
    y1[:bsz] = y_mine
    y1[bsz:] = y_pair


def third_kernel(facts, f0, f1, f2, f3, g0, g1, g2, g3, y0, t, y, ya, yb, yc, out, diag, y_all, link):
    bsz = out.shape[0]
    p = lax.axis_index("row")
    c = lax.axis_index("col")
    rows = [[f0, f1, f2, f3], [g0, g1, g2, g3]]
    take_diagonal(p, c, facts[MASK], rows, diag, bsz)
    acc = update(facts, rows, [y, ya, yb, yc], coset_picks(facts[MASK]), y_all, link, bsz)
    y2, _ = solve_pair(facts, diag, 2, t[:bsz] - acc[:bsz], t[bsz:] - acc[bsz:])
    out[...] = y0[:bsz] + y[:bsz] + y2


def call(kernel, n_smem, args, outs, scratch):
    return pl.pallas_call(
        kernel,
        in_specs=[SMEM] * n_smem + [VMEM] * (len(args) - n_smem),
        out_specs=[spec for spec, _ in outs],
        out_shape=[shape for _, shape in outs],
        scratch_shapes=scratch,
        compiler_params=pltpu.CompilerParams(vmem_limit_bytes=32 * 1024 * 1024),
    )(*args)


def pair_body(factor, rhs, parent, bounds, slot, structure, n_row, n_col):
    bsz, wide = rhs.shape
    f32 = jnp.float32

    def send(value, row_mask, col_mask):
        pairs = [
            (r * n_col + k, (r ^ row_mask) * n_col + (k ^ col_mask)) for r in range(n_row) for k in range(n_col)
        ]
        return lax.ppermute(value, ("row", "col"), pairs)

    def array(*shape):
        return (VMEM, jax.ShapeDtypeStruct(shape, f32))

    f0 = factor
    f2 = send(f0, 0, 2)
    facts, packed = call(
        facts_kernel,
        4,
        [parent, bounds, slot, structure, factor, rhs],
        [(SMEM, jax.ShapeDtypeStruct((FACTS,), jnp.int32)), array(bsz, 2 * bsz + wide)],
        [pltpu.SMEM((8,), jnp.int32)],
    )
    m = facts[MASK]
    g0, g2 = lax.switch(
        m - 1,
        [lambda a, b, k=k: (send(a, k, 0), send(b, k, 2)) for k in range(1, n_row)],
        packed,
        f0,
    )
    f1, f3, g1, g3 = [send(v, 0, 1) for v in (f0, f2, g0, g2)]
    rows = [f0, f1, f2, f3, g0, g1, g2, g3]

    diag = pltpu.VMEM((2, 2, bsz, bsz), f32)
    y_all = pltpu.VMEM((n_row * bsz, wide), f32)
    link = pltpu.VMEM((2 * bsz, n_row * bsz), f32)

    variant = jnp.where(m >= 4, 0, jnp.where(m == 1, 1, 2))

    def spread(y):
        return lax.switch(
            variant,
            [lambda v, ks=ks: tuple(send(v, k, 0) for k in ks) for ks in ((1, 2, 3), (2, 4, 6), (1, 4, 5))],
            y,
        )

    (y0,) = call(first_kernel, 1, [facts, rhs] + rows, [array(2 * bsz, wide)], [diag])
    y1, t = call(
        second_kernel,
        1,
        [facts, rhs] + rows + [y0, *spread(y0)],
        [array(2 * bsz, wide), array(2 * bsz, wide)],
        [diag, y_all, link],
    )
    (out,) = call(
        third_kernel,
        1,
        [facts] + rows + [y0, t, y1, *spread(y1)],
        [array(bsz, wide)],
        [diag, y_all, link],
    )
    return out


def body(factor, rhs, parent, bounds, slot, structure, n_row, n_col):
    count = slot.shape[0]
    pairs = count == 8 and n_row == 8 and n_col == 4 and bounds.shape[0] == 8
    if pairs:
        return pair_body(factor, rhs, parent, bounds, slot, structure, n_row, n_col)
    return general_body(factor, rhs, parent, bounds, slot, structure, n_row)


def solution(mesh):
    in_specs = (P("row", "col"), P("row", "col"), P(), P(), P(), P())
    out_specs = P("row", "col")
    step = functools.partial(body, n_row=mesh.shape["row"], n_col=mesh.shape["col"])
    return jax.shard_map(step, mesh=mesh, in_specs=in_specs, out_specs=out_specs, check_vma=False)
```

```python
import functools
import itertools

import jax
import jax.numpy as jnp
import numpy as np
from jax import lax
from jax.experimental import pallas as pl
from jax.experimental.pallas import tpu as pltpu
from jax.sharding import PartitionSpec as P

SMEM = pl.BlockSpec(memory_space=pltpu.SMEM)
VMEM = pl.BlockSpec(memory_space=pltpu.VMEM)
HIGHEST = lax.Precision.HIGHEST


def block_masks(parent, bounds, slot, structure):
    count = slot.shape[0]
    ar = jnp.arange(count, dtype=jnp.int32)
    logical = jnp.sum(jnp.where(slot[:, None] == ar[None, :], ar[:, None], 0), axis=0)
    node = jnp.sum((logical[:, None] >= bounds[None, 1:7]).astype(jnp.int32), axis=1)
    level = (node >= 4).astype(jnp.int32) + (node >= 6).astype(jnp.int32)
    nodes = jnp.arange(7, dtype=jnp.int32)
    grand = parent[parent]
    ancestor = ((nodes[None, :] == parent[:, None]) | (nodes[None, :] == grand[:, None])) & (
        nodes[None, :] != nodes[:, None]
    )
    node_hot = (node[:, None] == nodes[None, :]).astype(jnp.float32)
    perm_hot = (logical[:, None] == ar[None, :]).astype(jnp.float32)
    listed_store = jnp.dot(structure.astype(jnp.float32), perm_hot.T, precision=HIGHEST)
    anc_pairs = jnp.dot(
        node_hot, jnp.dot(ancestor.astype(jnp.float32), node_hot.T, precision=HIGHEST), precision=HIGHEST
    )
    list_pairs = jnp.dot(node_hot, listed_store, precision=HIGHEST)
    link = (anc_pairs * list_pairs).T > 0.5
    same = node[:, None] == node[None, :]
    return level, same, link


def masked(block_rows, mask):
    rblocks, width = mask.shape
    bsz = block_rows.shape[0] // rblocks
    shaped = block_rows.reshape(rblocks, bsz, width, bsz) * mask[:, None, :, None].astype(jnp.float32)
    return shaped.reshape(block_rows.shape)


def general_body(factor, rhs, parent, bounds, slot, structure, n_row):
    level, same, link = block_masks(parent, bounds, slot, structure)
    held = slot.shape[0] // n_row
    bsz = factor.shape[0] // held
    first = lax.axis_index("row") * held
    level_mine = lax.dynamic_slice_in_dim(level, first, held, 0)
    same_mine = lax.dynamic_slice_in_dim(same, first, held, 0)
    link_mine = lax.dynamic_slice_in_dim(link, first, held, 0)
    full_rows = lax.all_gather(factor, "col", axis=1, tiled=True)
    diag_part = masked(full_rows, same_mine)
    link_part = masked(full_rows, link_mine)

    def product(matrix, vector):
        return jnp.dot(
            matrix,
            lax.all_gather(vector, "row", axis=0, tiled=True),
            precision=HIGHEST,
            preferred_element_type=jnp.float32,
        )

    acc = jnp.zeros(rhs.shape, jnp.float32)
    result = jnp.zeros(rhs.shape, jnp.float32)
    for section in range(3):
        rows = jnp.repeat(level_mine == section, bsz)[:, None]
        solved = jnp.where(rows, product(diag_part, rhs - acc), 0.0)
        result = result + solved
        if section < 2:
            acc = acc + product(link_part, solved)
    return result


COUPLE = 0
SPREAD = 3
SAME = 4
LEVEL = 5
LINK0 = 8
LINK1 = 16
PICK = 20
FACTS = 24


def mask_sets():
    sets = [s for size in (2, 3) for s in itertools.combinations(range(1, 8), size)]
    sets += [s for s in itertools.combinations(range(1, 8), 4) if s[0] ^ s[1] ^ s[2] ^ s[3] == 0]
    table = np.zeros(256, np.int32)
    for i, s in enumerate(sets):
        table[sum(1 << k for k in s)] = i
    return sets, table


def as_int(flag):
    return jnp.where(flag, jnp.int32(1), jnp.int32(0))


def facts_kernel(parent_in, bounds_in, slot_in, structure_in, table_in, facts, parent, bounds, slot, structure, table, logical, node, sems):
    pairs = [(parent_in, parent), (bounds_in, bounds), (slot_in, slot), (structure_in, structure), (table_in, table)]
    copies = [pltpu.make_async_copy(a, b, sems.at[i]) for i, (a, b) in enumerate(pairs)]
    for copy in copies:
        copy.start()
    for copy in copies:
        copy.wait()
    p = lax.axis_index("row")
    c = lax.axis_index("col")
    wide = jnp.int32(0)
    for s in range(1, 7):
        wide = wide + as_int(bounds[s] == s)
    m = slot[wide] ^ slot[wide + 1]
    wide_level = as_int(wide >= 4) + as_int(wide >= 6)
    for i in range(8):
        q = slot[i]
        logical[q] = i
        node[q] = i - as_int(i > wide)
    for k in range(3):
        facts[COUPLE + k] = jnp.where(wide_level == k, m, 0)
    mine = node[p]
    facts[SAME] = as_int(node[p ^ m] == mine)
    level = as_int(mine >= 4) + as_int(mine >= 6)
    facts[LEVEL] = level
    place = logical[p]

    def linked(q):
        below = node[q]
        up = parent[below]
        top = parent[up]
        above = ((mine == up) | (mine == top)) & (mine != below)
        return as_int(above & (structure[below, place] == 1))

    for k in range(8):
        q = k ^ (2 * c)
        facts[LINK0 + k] = linked(q) * as_int(node[q] < 4)
    bits = jnp.int32(0)
    for i in range(4, 7):
        for j in range(6, 8):
            one = (node[slot[i]] >= 4) & (node[slot[i]] < 6)
            two = node[slot[j]] >= 6
            bits = bits | jnp.where(one & two, jnp.int32(1) << (slot[i] ^ slot[j]), 0)
    facts[SPREAD] = table[bits]
    for k in range(4):
        facts[PICK + k] = 0
        facts[LINK1 + k] = 0
    count = jnp.int32(0)
    for k in range(1, 8):
        on = (bits >> k) & 1
        at = jnp.minimum(count, 3)

        @pl.when(on == 1)
        def _(k=k, at=at):
            q = p ^ k
            facts[PICK + at] = k
            facts[LINK1 + at] = linked(q) * as_int((node[q] >= 4) & (node[q] < 6))

        count = count + on


def dot(a, b):
    return jnp.dot(a, b, precision=HIGHEST, preferred_element_type=jnp.float32)


def solve(facts, diag, section, mine, partner):
    same = facts[SAME].astype(jnp.float32)
    on = (facts[LEVEL] == section).astype(jnp.float32)
    return (dot(diag[0], mine) + same * dot(diag[1], partner)) * on


def partner_mask(facts):
    return facts[COUPLE] + facts[COUPLE + 1] + facts[COUPLE + 2]


def first_kernel(facts, rhs, partner, f0, f1, f2, f3, y, diag):
    bsz = rhs.shape[0]
    p = lax.axis_index("row")
    c = lax.axis_index("col")
    pieces = [f0, f1, f2, f3]
    for s in range(2):
        place = p ^ (2 * c)
        if s == 1:
            place = place ^ partner_mask(facts)
        for k in range(8):

            @pl.when(place == k)
            def _(s=s, k=k):
                at = (k % 2) * bsz
                diag[s] = pieces[k // 2][:, at : at + bsz]

    y[...] = solve(facts, diag, 0, rhs[...], partner[...])


def residual(facts, rhs, f0, f1, f2, f3, ys, y_all, link):
    bsz = rhs.shape[0]
    p = lax.axis_index("row")
    c = lax.axis_index("col")
    pieces = [f0, f1, f2, f3]
    for k, y in enumerate(ys):
        place = p ^ k ^ (2 * c)
        y_all[pl.ds(pl.multiple_of(place * bsz, bsz), bsz), :] = y[...]
    for k in range(8):
        at = (k % 2) * bsz
        on = facts[LINK0 + k].astype(jnp.float32)
        link[:, k * bsz : (k + 1) * bsz] = pieces[k // 2][:, at : at + bsz] * on
    return rhs[...] - dot(link[...], y_all[...])


def second_kernel(facts, rhs, f0, f1, f2, f3, diag, *rest):
    ys, (t, y, y_all, link) = rest[:8], rest[8:]
    t[...] = residual(facts, rhs, f0, f1, f2, f3, ys, y_all, link)
    y[...] = solve(facts, diag, 1, t[...], t[...])


def residual_kernel(facts, rhs, f0, f1, f2, f3, *rest):
    ys, (t, y_all, link) = rest[:8], rest[8:]
    t[...] = residual(facts, rhs, f0, f1, f2, f3, ys, y_all, link)


def solve_kernel(facts, diag, t, partner, y):
    y[...] = solve(facts, diag, 1, t[...], partner[...])


def last_residual(facts, f0, f1, f2, f3, t, ys, total, block):
    bsz = t.shape[0]
    p = lax.axis_index("row")
    c = lax.axis_index("col")
    pieces = [f0, f1, f2, f3]
    total[...] = t[...]
    for s, y in enumerate(ys):

        @pl.when(facts[LINK1 + s] == 1)
        def _(s=s, y=y):
            place = p ^ facts[PICK + s] ^ (2 * c)
            for k in range(8):

                @pl.when(place == k)
                def _(k=k):
                    at = (k % 2) * bsz
                    block[...] = pieces[k // 2][:, at : at + bsz]

            total[...] -= dot(block[...], y[...])


def third_kernel(facts, f0, f1, f2, f3, diag, t, y0, y1, z0, z1, z2, z3, out, total, block):
    last_residual(facts, f0, f1, f2, f3, t, [z0, z1, z2, z3], total, block)
    out[...] = y0[...] + y1[...] + solve(facts, diag, 2, total[...], total[...])


def last_residual_kernel(facts, f0, f1, f2, f3, t, z0, z1, z2, z3, total, block):
    last_residual(facts, f0, f1, f2, f3, t, [z0, z1, z2, z3], total, block)


def last_solve_kernel(facts, diag, t, partner, y0, y1, out):
    out[...] = y0[...] + y1[...] + solve(facts, diag, 2, t[...], partner[...])


def call(kernel, args, outs, scratch=()):
    return pl.pallas_call(
        kernel,
        in_specs=[SMEM] + [VMEM] * (len(args) - 1),
        out_specs=[VMEM] * len(outs),
        out_shape=[jax.ShapeDtypeStruct(shape, jnp.float32) for shape in outs],
        scratch_shapes=[pltpu.VMEM(shape, jnp.float32) for shape in scratch],
        compiler_params=pltpu.CompilerParams(vmem_limit_bytes=32 * 1024 * 1024),
    )(*args)


def find_facts(parent, bounds, slot, structure, table):
    i32 = jnp.int32
    args = [parent, bounds, slot, structure, jnp.asarray(table)]
    return pl.pallas_call(
        facts_kernel,
        in_specs=[pl.BlockSpec(memory_space=pl.ANY)] * 5,
        out_specs=SMEM,
        out_shape=jax.ShapeDtypeStruct((FACTS,), i32),
        scratch_shapes=[pltpu.SMEM(a.shape, i32) for a in args]
        + [pltpu.SMEM((8,), i32), pltpu.SMEM((8,), i32), pltpu.SemaphoreType.DMA((5,))],
    )(*args)


def wide_body(factor, rhs, parent, bounds, slot, structure, n_row, n_col):
    bsz, cols = rhs.shape
    block = (bsz, cols)
    square = (bsz, bsz)
    sets, table = mask_sets()

    def send(value, row_mask, col_mask=0):
        pairs = [
            (r * n_col + k, (r ^ row_mask) * n_col + (k ^ col_mask)) for r in range(n_row) for k in range(n_col)
        ]
        return lax.ppermute(value, ("row", "col"), pairs)

    facts = find_facts(parent, bounds, slot, structure, table)

    def before(factor, rhs, mask):
        f2 = send(factor, 0, 2)
        partner = send(rhs, mask) if mask else rhs
        f1 = send(factor, 0, 1)
        f3 = send(f2, 0, 1)
        return f1, f2, f3, partner

    f1, f2, f3, partner = lax.switch(
        facts[COUPLE], [functools.partial(before, mask=k) for k in range(n_row)], factor, rhs
    )
    rows = [factor, f1, f2, f3]
    y0, diag = call(first_kernel, [facts, rhs, partner] + rows, [block, (2, bsz, bsz)])

    far = send(y0, 4)
    near = [send(y0, k) for k in (1, 2, 3)]
    ys = [y0] + near + [far] + [send(far, k) for k in (1, 2, 3)]

    def middle(mask, *args):
        facts, rhs, f0, f1, f2, f3, diag, *ys = args
        wide = (bsz, n_row * bsz)
        tall = (n_row * bsz, cols)
        if not mask:
            return tuple(call(second_kernel, args, [block, block], [tall, wide]))
        (t,) = call(residual_kernel, [facts, rhs, f0, f1, f2, f3] + ys, [block], [tall, wide])
        (y,) = call(solve_kernel, [facts, diag, t, send(t, mask)], [block])
        return t, y

    t, y1 = lax.switch(
        facts[COUPLE + 1],
        [functools.partial(middle, k) for k in range(n_row)],
        *([facts, rhs] + rows + [diag] + ys),
    )

    def spread(masks, y):
        return tuple(send(y, k) for k in masks) + (y,) * (4 - len(masks))

    zs = lax.switch(facts[SPREAD], [functools.partial(spread, s) for s in sets], y1)

    def end(mask, *args):
        facts, f0, f1, f2, f3, diag, t, y0, y1, *zs = args
        if not mask:
            return call(third_kernel, args, [block], [block, square])[0]
        (t2,) = call(last_residual_kernel, [facts, f0, f1, f2, f3, t] + zs, [block], [square])
        return call(last_solve_kernel, [facts, diag, t2, send(t2, mask), y0, y1], [block])[0]

    return lax.switch(
        facts[COUPLE + 2],
        [functools.partial(end, k) for k in range(n_row)],
        *([facts] + rows + [diag, t, y0, y1, *zs]),
    )


def body(factor, rhs, parent, bounds, slot, structure, n_row, n_col):
    count = slot.shape[0]
    if count == 8 and n_row == 8 and n_col == 4 and bounds.shape[0] == 8:
        return wide_body(factor, rhs, parent, bounds, slot, structure, n_row, n_col)
    return general_body(factor, rhs, parent, bounds, slot, structure, n_row)


def solution(mesh):
    in_specs = (P("row", "col"), P("row", "col"), P(), P(), P(), P())
    out_specs = P("row", "col")
    step = functools.partial(body, n_row=mesh.shape["row"], n_col=mesh.shape["col"])
    return jax.shard_map(step, mesh=mesh, in_specs=in_specs, out_specs=out_specs, check_vma=False)
```

```python
import functools
import itertools

import jax
import jax.numpy as jnp
import numpy as np
from jax import lax
from jax.experimental import pallas as pl
from jax.experimental.pallas import tpu as pltpu
from jax.sharding import PartitionSpec as P

SMEM = pl.BlockSpec(memory_space=pltpu.SMEM)
VMEM = pl.BlockSpec(memory_space=pltpu.VMEM)
HIGHEST = lax.Precision.HIGHEST


def block_masks(parent, bounds, slot, structure):
    count = slot.shape[0]
    ar = jnp.arange(count, dtype=jnp.int32)
    logical = jnp.sum(jnp.where(slot[:, None] == ar[None, :], ar[:, None], 0), axis=0)
    node = jnp.sum((logical[:, None] >= bounds[None, 1:7]).astype(jnp.int32), axis=1)
    level = (node >= 4).astype(jnp.int32) + (node >= 6).astype(jnp.int32)
    nodes = jnp.arange(7, dtype=jnp.int32)
    grand = parent[parent]
    ancestor = ((nodes[None, :] == parent[:, None]) | (nodes[None, :] == grand[:, None])) & (
        nodes[None, :] != nodes[:, None]
    )
    node_hot = (node[:, None] == nodes[None, :]).astype(jnp.float32)
    perm_hot = (logical[:, None] == ar[None, :]).astype(jnp.float32)
    listed_store = jnp.dot(structure.astype(jnp.float32), perm_hot.T, precision=HIGHEST)
    anc_pairs = jnp.dot(
        node_hot, jnp.dot(ancestor.astype(jnp.float32), node_hot.T, precision=HIGHEST), precision=HIGHEST
    )
    list_pairs = jnp.dot(node_hot, listed_store, precision=HIGHEST)
    link = (anc_pairs * list_pairs).T > 0.5
    same = node[:, None] == node[None, :]
    return level, same, link


def masked(block_rows, mask):
    rblocks, width = mask.shape
    bsz = block_rows.shape[0] // rblocks
    shaped = block_rows.reshape(rblocks, bsz, width, bsz) * mask[:, None, :, None].astype(jnp.float32)
    return shaped.reshape(block_rows.shape)


def general_body(factor, rhs, parent, bounds, slot, structure, n_row):
    level, same, link = block_masks(parent, bounds, slot, structure)
    held = slot.shape[0] // n_row
    bsz = factor.shape[0] // held
    first = lax.axis_index("row") * held
    level_mine = lax.dynamic_slice_in_dim(level, first, held, 0)
    same_mine = lax.dynamic_slice_in_dim(same, first, held, 0)
    link_mine = lax.dynamic_slice_in_dim(link, first, held, 0)
    full_rows = lax.all_gather(factor, "col", axis=1, tiled=True)
    diag_part = masked(full_rows, same_mine)
    link_part = masked(full_rows, link_mine)

    def product(matrix, vector):
        return jnp.dot(
            matrix,
            lax.all_gather(vector, "row", axis=0, tiled=True),
            precision=HIGHEST,
            preferred_element_type=jnp.float32,
        )

    acc = jnp.zeros(rhs.shape, jnp.float32)
    result = jnp.zeros(rhs.shape, jnp.float32)
    for section in range(3):
        rows = jnp.repeat(level_mine == section, bsz)[:, None]
        solved = jnp.where(rows, product(diag_part, rhs - acc), 0.0)
        result = result + solved
        if section < 2:
            acc = acc + product(link_part, solved)
    return result


FIRST = 0
MIDDLE = 1
SPREAD = 2
END = 3
SAME = 4
LEVEL = 5
PARTNER = 6
LINK0 = 8
LINK1 = 16
PICK = 20
FACTS = 24

MASK_PAIRS = list(itertools.combinations(range(1, 8), 2))


def mask_table():
    table = np.zeros((8, 8), np.int32)
    for i, (u, v) in enumerate(MASK_PAIRS):
        table[u, v] = table[v, u] = i
    return table


def as_int(flag):
    return jnp.where(flag, jnp.int32(1), jnp.int32(0))


def facts_kernel(parent_in, bounds_in, slot_in, structure_in, table_in, facts, parent, bounds, slot, structure, table, logical, node, sems):
    pairs = [(parent_in, parent), (bounds_in, bounds), (slot_in, slot), (structure_in, structure), (table_in, table)]
    copies = [pltpu.make_async_copy(a, b, sems.at[i]) for i, (a, b) in enumerate(pairs)]
    for copy in copies:
        copy.start()
    for copy in copies:
        copy.wait()
    p = lax.axis_index("row")
    c = lax.axis_index("col")
    wide = jnp.int32(0)
    for s in range(1, 7):
        wide = wide + as_int(bounds[s] == s)
    m = slot[wide] ^ slot[wide + 1]
    wide_level = as_int(wide >= 4) + as_int(wide >= 6)
    for i in range(8):
        q = slot[i]
        logical[q] = i
        node[q] = i - as_int(i > wide)
    mine = node[p]
    place = logical[p]
    level = as_int(mine >= 4) + as_int(mine >= 6)
    facts[FIRST] = jnp.where(wide_level == 0, m, 0)
    facts[MIDDLE] = jnp.where(wide_level == 1, m, 0)
    facts[SAME] = as_int(node[p ^ m] == mine)
    facts[LEVEL] = level
    facts[PARTNER] = m

    def linked(q):
        below = node[q]
        up = parent[below]
        top = parent[up]
        above = ((mine == up) | (mine == top)) & (mine != below)
        return as_int(above & (structure[below, place] == 1))

    for k in range(8):
        q = k ^ (2 * c)
        facts[LINK0 + k] = linked(q) * as_int(node[q] < 4)
    top = slot[7]
    u = slot[jnp.where(wide_level == 2, 4, 5)] ^ top
    v = slot[jnp.where(wide_level == 2, 5, 6)] ^ top
    third = slot[4] ^ top
    facts[SPREAD] = table[u, v]
    low = jnp.minimum(u, v)
    high = jnp.maximum(u, v)
    facts[END] = jnp.where(wide_level == 1, third, jnp.where(wide_level == 2, 7 + m, 0))
    at_two = wide_level == 2
    picks = [low, high, jnp.where(at_two, low ^ m, third), high ^ m]
    fresh = [True, True, wide_level >= 1, at_two]
    for k in range(4):
        q = p ^ picks[k]
        on = linked(q) * as_int((node[q] >= 4) & (node[q] < 6) & fresh[k])
        for j in range(min(k, 2)):
            on = on * as_int(picks[k] != picks[j])
        facts[PICK + k] = picks[k]
        facts[LINK1 + k] = on


def dot(a, b):
    return jnp.dot(a, b, precision=HIGHEST, preferred_element_type=jnp.float32)


def solve(facts, diag, section, mine, partner, y):
    on = facts[LEVEL] == section
    y[...] = dot(diag[0], mine[...]) * on.astype(jnp.float32)

    @pl.when(on & (facts[SAME] == 1))
    def _():
        y[...] += dot(diag[1], partner[...])


def first_kernel(facts, rhs, partner, f0, f1, f2, f3, y, diag):
    bsz = rhs.shape[0]
    p = lax.axis_index("row")
    c = lax.axis_index("col")
    pieces = [f0, f1, f2, f3]
    for s in range(2):
        place = p ^ (2 * c)
        if s == 1:
            place = place ^ facts[PARTNER]
        for k in range(8):

            @pl.when(place == k)
            def _(s=s, k=k):
                at = (k % 2) * bsz
                diag[s] = pieces[k // 2][:, at : at + bsz]

    solve(facts, diag, 0, rhs, partner, y)


def unread_kernel(out):
    del out


def residual(facts, rhs, f0, f1, f2, f3, ys, y_all, link):
    bsz = rhs.shape[0]
    p = lax.axis_index("row")
    c = lax.axis_index("col")
    pieces = [f0, f1, f2, f3]
    for k, y in enumerate(ys):
        place = p ^ k ^ (2 * c)
        y_all[pl.ds(pl.multiple_of(place * bsz, bsz), bsz), :] = y[...]
    for k in range(8):
        at = (k % 2) * bsz
        on = facts[LINK0 + k].astype(jnp.float32)
        link[:, k * bsz : (k + 1) * bsz] = pieces[k // 2][:, at : at + bsz] * on
    return rhs[...] - dot(link[...], y_all[...])


def second_kernel(facts, rhs, f0, f1, f2, f3, diag, *rest):
    ys, (t, y, y_all, link) = rest[:8], rest[8:]
    t[...] = residual(facts, rhs, f0, f1, f2, f3, ys, y_all, link)
    solve(facts, diag, 1, t, t, y)


def residual_kernel(facts, rhs, f0, f1, f2, f3, *rest):
    ys, (t, y_all, link) = rest[:8], rest[8:]
    t[...] = residual(facts, rhs, f0, f1, f2, f3, ys, y_all, link)


def solve_kernel(facts, diag, t, partner, y):
    solve(facts, diag, 1, t, partner, y)


def last_residual(facts, f0, f1, f2, f3, t, zs, total, block):
    bsz = t.shape[0]
    p = lax.axis_index("row")
    c = lax.axis_index("col")
    pieces = [f0, f1, f2, f3]
    total[...] = t[...]
    for s, z in enumerate(zs):

        @pl.when(facts[LINK1 + s] == 1)
        def _(s=s, z=z):
            place = p ^ facts[PICK + s] ^ (2 * c)
            for k in range(8):

                @pl.when(place == k)
                def _(k=k):
                    at = (k % 2) * bsz
                    block[...] = pieces[k // 2][:, at : at + bsz]

            total[...] -= dot(block[...], z[...])


def third_kernel(facts, f0, f1, f2, f3, diag, t, y0, y1, *rest):
    zs, (out, total, block) = rest[:-3], rest[-3:]
    last_residual(facts, f0, f1, f2, f3, t, zs, total, block)
    solve(facts, diag, 2, total, total, out)
    out[...] += y0[...] + y1[...]


def last_residual_kernel(facts, f0, f1, f2, f3, t, z0, z1, z2, z3, total, block):
    last_residual(facts, f0, f1, f2, f3, t, [z0, z1, z2, z3], total, block)


def last_solve_kernel(facts, diag, t, partner, y0, y1, out):
    solve(facts, diag, 2, t, partner, out)
    out[...] += y0[...] + y1[...]


def call(kernel, args, outs, scratch=()):
    return pl.pallas_call(
        kernel,
        in_specs=[SMEM] + [VMEM] * (len(args) - 1),
        out_specs=[VMEM] * len(outs),
        out_shape=[jax.ShapeDtypeStruct(shape, jnp.float32) for shape in outs],
        scratch_shapes=[pltpu.VMEM(shape, jnp.float32) for shape in scratch],
        compiler_params=pltpu.CompilerParams(vmem_limit_bytes=32 * 1024 * 1024),
    )(*args)


def find_facts(parent, bounds, slot, structure, table):
    i32 = jnp.int32
    args = [parent, bounds, slot, structure, jnp.asarray(table)]
    return pl.pallas_call(
        facts_kernel,
        in_specs=[pl.BlockSpec(memory_space=pl.ANY)] * 5,
        out_specs=SMEM,
        out_shape=jax.ShapeDtypeStruct((FACTS,), i32),
        scratch_shapes=[pltpu.SMEM(a.shape, i32) for a in args]
        + [pltpu.SMEM((8,), i32), pltpu.SMEM((8,), i32), pltpu.SemaphoreType.DMA((5,))],
    )(*args)


def wide_body(factor, rhs, parent, bounds, slot, structure, n_row, n_col):
    bsz, cols = rhs.shape
    block = (bsz, cols)
    square = (bsz, bsz)

    def send(value, row_mask, col_mask=0):
        pairs = [
            (r * n_col + k, (r ^ row_mask) * n_col + (k ^ col_mask)) for r in range(n_row) for k in range(n_col)
        ]
        return lax.ppermute(value, ("row", "col"), pairs)

    f2 = send(factor, 0, 2)
    f1 = send(factor, 0, 1)
    facts = find_facts(parent, bounds, slot, structure, mask_table())
    f3 = send(f2, 0, 1)

    def first_partner(mask, value):
        if mask:
            return send(value, mask)
        return pl.pallas_call(unread_kernel, out_specs=VMEM, out_shape=jax.ShapeDtypeStruct(block, jnp.float32))()

    partner = lax.switch(facts[FIRST], [functools.partial(first_partner, k) for k in range(n_row)], rhs)
    rows = [factor, f1, f2, f3]
    y0, diag = call(first_kernel, [facts, rhs, partner] + rows, [block, (2, bsz, bsz)])

    far = send(y0, 4)
    near = [send(y0, k) for k in (1, 2, 3)]
    ys = [y0] + near + [far] + [send(far, k) for k in (1, 2, 3)]

    def middle(mask, *args):
        facts, rhs, f0, f1, f2, f3, diag, *ys = args
        wide = (bsz, n_row * bsz)
        tall = (n_row * bsz, cols)
        if not mask:
            return tuple(call(second_kernel, args, [block, block], [tall, wide]))
        (t,) = call(residual_kernel, [facts, rhs, f0, f1, f2, f3] + ys, [block], [tall, wide])
        (y,) = call(solve_kernel, [facts, diag, t, send(t, mask)], [block])
        return t, y

    t, y1 = lax.switch(
        facts[MIDDLE],
        [functools.partial(middle, k) for k in range(n_row)],
        *([facts, rhs] + rows + [diag] + ys),
    )

    zs = lax.switch(
        facts[SPREAD],
        [lambda y, u=u, v=v: (send(y, u), send(y, v)) for u, v in MASK_PAIRS],
        y1,
    )

    def end(mask, level, *args):
        facts, f0, f1, f2, f3, diag, t, y0, y1, z0, z1 = args
        if not mask:
            return call(third_kernel, args, [block], [block, square])[0]
        if level == 1:
            return call(third_kernel, args + (send(y1, mask),), [block], [block, square])[0]
        zs = [z0, z1, send(z0, mask), send(z1, mask)]
        (t2,) = call(last_residual_kernel, [facts, f0, f1, f2, f3, t] + zs, [block], [square])
        return call(last_solve_kernel, [facts, diag, t2, send(t2, mask), y0, y1], [block])[0]

    return lax.switch(
        facts[END],
        [functools.partial(end, k, 1) for k in range(n_row)] + [functools.partial(end, k, 2) for k in range(1, n_row)],
        *([facts] + rows + [diag, t, y0, y1, *zs]),
    )


def body(factor, rhs, parent, bounds, slot, structure, n_row, n_col):
    count = slot.shape[0]
    if count == 8 and n_row == 8 and n_col == 4 and bounds.shape[0] == 8:
        return wide_body(factor, rhs, parent, bounds, slot, structure, n_row, n_col)
    return general_body(factor, rhs, parent, bounds, slot, structure, n_row)


def solution(mesh):
    in_specs = (P("row", "col"), P("row", "col"), P(), P(), P(), P())
    out_specs = P("row", "col")
    step = functools.partial(body, n_row=mesh.shape["row"], n_col=mesh.shape["col"])
    return jax.shard_map(step, mesh=mesh, in_specs=in_specs, out_specs=out_specs, check_vma=False)
```

```python
import functools
import itertools

import jax
import jax.numpy as jnp
import numpy as np
from jax import lax
from jax.experimental import pallas as pl
from jax.experimental.pallas import tpu as pltpu
from jax.sharding import PartitionSpec as P

SMEM = pl.BlockSpec(memory_space=pltpu.SMEM)
VMEM = pl.BlockSpec(memory_space=pltpu.VMEM)
HBM = pl.BlockSpec(memory_space=pltpu.HBM)
HIGHEST = lax.Precision.HIGHEST
SMALL = pltpu.CompilerParams(vmem_limit_bytes=4 * 1024 * 1024)


def block_masks(parent, bounds, slot, structure):
    count = slot.shape[0]
    ar = jnp.arange(count, dtype=jnp.int32)
    logical = jnp.sum(jnp.where(slot[:, None] == ar[None, :], ar[:, None], 0), axis=0)
    node = jnp.sum((logical[:, None] >= bounds[None, 1:7]).astype(jnp.int32), axis=1)
    level = (node >= 4).astype(jnp.int32) + (node >= 6).astype(jnp.int32)
    nodes = jnp.arange(7, dtype=jnp.int32)
    grand = parent[parent]
    ancestor = ((nodes[None, :] == parent[:, None]) | (nodes[None, :] == grand[:, None])) & (
        nodes[None, :] != nodes[:, None]
    )
    node_hot = (node[:, None] == nodes[None, :]).astype(jnp.float32)
    perm_hot = (logical[:, None] == ar[None, :]).astype(jnp.float32)
    listed_store = jnp.dot(structure.astype(jnp.float32), perm_hot.T, precision=HIGHEST)
    anc_pairs = jnp.dot(
        node_hot, jnp.dot(ancestor.astype(jnp.float32), node_hot.T, precision=HIGHEST), precision=HIGHEST
    )
    list_pairs = jnp.dot(node_hot, listed_store, precision=HIGHEST)
    link = (anc_pairs * list_pairs).T > 0.5
    same = node[:, None] == node[None, :]
    return level, same, link


def masked(block_rows, mask):
    rblocks, width = mask.shape
    bsz = block_rows.shape[0] // rblocks
    shaped = block_rows.reshape(rblocks, bsz, width, bsz) * mask[:, None, :, None].astype(jnp.float32)
    return shaped.reshape(block_rows.shape)


def general_body(factor, rhs, parent, bounds, slot, structure, n_row):
    level, same, link = block_masks(parent, bounds, slot, structure)
    held = slot.shape[0] // n_row
    bsz = factor.shape[0] // held
    first = lax.axis_index("row") * held
    level_mine = lax.dynamic_slice_in_dim(level, first, held, 0)
    same_mine = lax.dynamic_slice_in_dim(same, first, held, 0)
    link_mine = lax.dynamic_slice_in_dim(link, first, held, 0)
    full_rows = lax.all_gather(factor, "col", axis=1, tiled=True)
    diag_part = masked(full_rows, same_mine)
    link_part = masked(full_rows, link_mine)

    def product(matrix, vector):
        return jnp.dot(
            matrix,
            lax.all_gather(vector, "row", axis=0, tiled=True),
            precision=HIGHEST,
            preferred_element_type=jnp.float32,
        )

    acc = jnp.zeros(rhs.shape, jnp.float32)
    result = jnp.zeros(rhs.shape, jnp.float32)
    for section in range(3):
        rows = jnp.repeat(level_mine == section, bsz)[:, None]
        solved = jnp.where(rows, product(diag_part, rhs - acc), 0.0)
        result = result + solved
        if section < 2:
            acc = acc + product(link_part, solved)
    return result


FIRST = 0
PARTNER = 1
SAME = 2
LEVEL = 3
HEAD = 8
MIDDLE = 0
SPREAD = 1
END = 2
LINK0 = 8
LINK1 = 16
PICK = 20
FACTS = 24

MASK_PAIRS = list(itertools.combinations(range(1, 8), 2))


def mask_table():
    table = np.zeros((8, 8), np.int32)
    for i, (u, v) in enumerate(MASK_PAIRS):
        table[u, v] = table[v, u] = i
    return table


def as_int(flag):
    return jnp.where(flag, jnp.int32(1), jnp.int32(0))


def fetch(pairs, sems):
    copies = [pltpu.make_async_copy(a, b, sems.at[i]) for i, (a, b) in enumerate(pairs)]
    for copy in copies:
        copy.start()
    for copy in copies:
        copy.wait()


def wide_block(bounds):
    wide = jnp.int32(0)
    for s in range(1, 7):
        wide = wide + as_int(bounds[s] == s)
    return wide


def level_of(node):
    return as_int(node >= 4) + as_int(node >= 6)


def head_kernel(bounds_in, slot_in, head, bounds, slot, sems):
    fetch([(bounds_in, bounds), (slot_in, slot)], sems)
    p = lax.axis_index("row")
    wide = wide_block(bounds)
    m = slot[wide] ^ slot[wide + 1]
    place = jnp.int32(0)
    for i in range(1, 8):
        place = place + i * as_int(slot[i] == p)
    node = place - as_int(place > wide)
    head[FIRST] = jnp.where(wide < 4, m, 0)
    head[PARTNER] = m
    head[SAME] = as_int(node == wide)
    head[LEVEL] = level_of(node)
    for k in range(4, HEAD):
        head[k] = 0


def facts_kernel(after, parent_in, bounds_in, slot_in, structure_in, table_in, facts, parent, bounds, slot, structure, table, logical, node, sems):
    del after
    pairs = [(parent_in, parent), (bounds_in, bounds), (slot_in, slot), (structure_in, structure), (table_in, table)]
    fetch(pairs, sems)
    p = lax.axis_index("row")
    c = lax.axis_index("col")
    wide = wide_block(bounds)
    wide_level = level_of(wide)
    m = slot[wide] ^ slot[wide + 1]
    for i in range(8):
        q = slot[i]
        logical[q] = i
        node[q] = i - as_int(i > wide)
    mine = node[p]
    place = logical[p]
    for k in range(3, LINK0):
        facts[k] = 0
    facts[MIDDLE] = jnp.where(wide_level == 1, m, 0)

    def linked(q):
        below = node[q]
        up = parent[below]
        top = parent[up]
        above = ((mine == up) | (mine == top)) & (mine != below)
        return as_int(above & (structure[below, place] == 1))

    for k in range(8):
        q = k ^ (2 * c)
        facts[LINK0 + k] = linked(q) * as_int(node[q] < 4)
    top = slot[7]
    u = slot[jnp.where(wide_level == 2, 4, 5)] ^ top
    v = slot[jnp.where(wide_level == 2, 5, 6)] ^ top
    third = slot[4] ^ top
    facts[SPREAD] = table[u, v]
    low = jnp.minimum(u, v)
    high = jnp.maximum(u, v)
    facts[END] = jnp.where(wide_level == 1, third, jnp.where(wide_level == 2, 7 + m, 0))
    at_two = wide_level == 2
    picks = [low, high, jnp.where(at_two, low ^ m, third), high ^ m]
    fresh = [True, True, wide_level >= 1, at_two]
    for k in range(4):
        q = p ^ picks[k]
        on = linked(q) * as_int((node[q] >= 4) & (node[q] < 6) & fresh[k])
        for j in range(min(k, 2)):
            on = on * as_int(picks[k] != picks[j])
        facts[PICK + k] = picks[k]
        facts[LINK1 + k] = on


def dot(a, b):
    return jnp.dot(a, b, precision=HIGHEST, preferred_element_type=jnp.float32)


def solve(head, diag, section, mine, partner, y):
    on = head[LEVEL] == section
    y[...] = dot(diag[0], mine[...]) * on.astype(jnp.float32)

    @pl.when(on & (head[SAME] == 1))
    def _():
        y[...] += dot(diag[1], partner[...])


def first_kernel(head, rhs, partner, f0, f1, f2, f3, y, diag):
    bsz = rhs.shape[0]
    p = lax.axis_index("row")
    c = lax.axis_index("col")
    pieces = [f0, f1, f2, f3]
    for s in range(2):
        place = p ^ (2 * c)
        if s == 1:
            place = place ^ head[PARTNER]
        for k in range(8):

            @pl.when(place == k)
            def _(s=s, k=k):
                at = (k % 2) * bsz
                diag[s] = pieces[k // 2][:, at : at + bsz]

    solve(head, diag, 0, rhs, partner, y)


def unread_kernel(out):
    del out


def residual(facts, rhs, f0, f1, f2, f3, ys, y_all, link):
    bsz = rhs.shape[0]
    p = lax.axis_index("row")
    c = lax.axis_index("col")
    pieces = [f0, f1, f2, f3]
    for k, y in enumerate(ys):
        place = p ^ k ^ (2 * c)
        y_all[pl.ds(pl.multiple_of(place * bsz, bsz), bsz), :] = y[...]
    for k in range(8):
        at = (k % 2) * bsz
        on = facts[LINK0 + k].astype(jnp.float32)
        link[:, k * bsz : (k + 1) * bsz] = pieces[k // 2][:, at : at + bsz] * on
    return rhs[...] - dot(link[...], y_all[...])


def residual_kernel(facts, rhs, f0, f1, f2, f3, *rest):
    ys, (t, y_all, link) = rest[:8], rest[8:]
    t[...] = residual(facts, rhs, f0, f1, f2, f3, ys, y_all, link)


def solve_kernel(head, diag, t, partner, y):
    solve(head, diag, 1, t, partner, y)


def last_residual(facts, f0, f1, f2, f3, t, zs, total, block):
    bsz = t.shape[0]
    p = lax.axis_index("row")
    c = lax.axis_index("col")
    pieces = [f0, f1, f2, f3]
    total[...] = t[...]
    for s, z in enumerate(zs):

        @pl.when(facts[LINK1 + s] == 1)
        def _(s=s, z=z):
            place = p ^ facts[PICK + s] ^ (2 * c)
            for k in range(8):

                @pl.when(place == k)
                def _(k=k):
                    at = (k % 2) * bsz
                    block[...] = pieces[k // 2][:, at : at + bsz]

            total[...] -= dot(block[...], z[...])


def third_kernel(head, facts, f0, f1, f2, f3, diag, t, y0, y1, *rest):
    zs, (out, total, block) = rest[:-3], rest[-3:]
    last_residual(facts, f0, f1, f2, f3, t, zs, total, block)
    solve(head, diag, 2, total, total, out)
    out[...] += y0[...] + y1[...]


def last_residual_kernel(facts, f0, f1, f2, f3, t, z0, z1, z2, z3, total, block):
    last_residual(facts, f0, f1, f2, f3, t, [z0, z1, z2, z3], total, block)


def last_solve_kernel(head, diag, t, partner, y0, y1, out):
    solve(head, diag, 2, t, partner, out)
    out[...] += y0[...] + y1[...]


def call(kernel, args, outs, scratch=(), n_smem=1):
    return pl.pallas_call(
        kernel,
        in_specs=[SMEM] * n_smem + [VMEM] * (len(args) - n_smem),
        out_specs=[VMEM] * len(outs),
        out_shape=[jax.ShapeDtypeStruct(shape, jnp.float32) for shape in outs],
        scratch_shapes=[pltpu.VMEM(shape, jnp.float32) for shape in scratch],
        compiler_params=SMALL,
    )(*args)


def find_head(bounds, slot):
    i32 = jnp.int32
    return pl.pallas_call(
        head_kernel,
        in_specs=[pl.BlockSpec(memory_space=pl.ANY)] * 2,
        out_specs=SMEM,
        out_shape=jax.ShapeDtypeStruct((HEAD,), i32),
        scratch_shapes=[pltpu.SMEM(bounds.shape, i32), pltpu.SMEM(slot.shape, i32), pltpu.SemaphoreType.DMA((2,))],
    )(bounds, slot)


def find_facts(after, parent, bounds, slot, structure, table):
    i32 = jnp.int32
    args = [parent, bounds, slot, structure, jnp.asarray(table)]
    return pl.pallas_call(
        facts_kernel,
        in_specs=[VMEM] + [HBM] * 5,
        out_specs=SMEM,
        out_shape=jax.ShapeDtypeStruct((FACTS,), i32),
        scratch_shapes=[pltpu.SMEM(a.shape, i32) for a in args]
        + [pltpu.SMEM((8,), i32), pltpu.SMEM((8,), i32), pltpu.SemaphoreType.DMA((5,))],
        compiler_params=SMALL,
    )(after, *args)


def wide_body(factor, rhs, parent, bounds, slot, structure, n_row, n_col):
    bsz, cols = rhs.shape
    block = (bsz, cols)
    square = (bsz, bsz)

    def send(value, row_mask, col_mask=0):
        pairs = [
            (r * n_col + k, (r ^ row_mask) * n_col + (k ^ col_mask)) for r in range(n_row) for k in range(n_col)
        ]
        return lax.ppermute(value, ("row", "col"), pairs)

    head = find_head(bounds, slot)
    factor, rhs, head = lax.optimization_barrier((factor, rhs, head))
    f0 = factor
    f2 = send(f0, 0, 2)
    f1 = send(f0, 0, 1)
    def first_partner(mask, value):
        if mask:
            return send(value, mask)
        shape = jax.ShapeDtypeStruct(block, jnp.float32)
        return pl.pallas_call(unread_kernel, out_specs=VMEM, out_shape=shape, compiler_params=SMALL)()

    partner = lax.switch(head[FIRST], [functools.partial(first_partner, k) for k in range(n_row)], rhs)
    f2, partner = lax.optimization_barrier((f2, partner))
    f3 = send(f2, 0, 1)
    rows = [f0, f1, f2, f3]
    y0, diag = call(first_kernel, [head, rhs, partner] + rows, [block, (2, bsz, bsz)])

    far = send(y0, 4)
    near = [send(y0, k) for k in (1, 2, 3)]
    ys = [y0] + near + [far] + [send(far, k) for k in (1, 2, 3)]
    facts = find_facts(y0, parent, bounds, slot, structure, mask_table())
    (t,) = call(residual_kernel, [facts, rhs] + rows + ys, [block], [(n_row * bsz, cols), (bsz, n_row * bsz)])

    def middle(mask, head, diag, t):
        partner = send(t, mask) if mask else t
        return call(solve_kernel, [head, diag, t, partner], [block])[0]

    y1 = lax.switch(facts[MIDDLE], [functools.partial(middle, k) for k in range(n_row)], head, diag, t)

    zs = lax.switch(
        facts[SPREAD],
        [lambda y, u=u, v=v: (send(y, u), send(y, v)) for u, v in MASK_PAIRS],
        y1,
    )

    def end(mask, level, *args):
        head, facts, f0, f1, f2, f3, diag, t, y0, y1, z0, z1 = args
        if not mask:
            return call(third_kernel, args, [block], [block, square], 2)[0]
        if level == 1:
            return call(third_kernel, args + (send(y1, mask),), [block], [block, square], 2)[0]
        zs = [z0, z1, send(z0, mask), send(z1, mask)]
        (t2,) = call(last_residual_kernel, [facts, f0, f1, f2, f3, t] + zs, [block], [square])
        return call(last_solve_kernel, [head, diag, t2, send(t2, mask), y0, y1], [block])[0]

    return lax.switch(
        facts[END],
        [functools.partial(end, k, 1) for k in range(n_row)] + [functools.partial(end, k, 2) for k in range(1, n_row)],
        *([head, facts] + rows + [diag, t, y0, y1, *zs]),
    )


def body(factor, rhs, parent, bounds, slot, structure, n_row, n_col):
    count = slot.shape[0]
    if count == 8 and n_row == 8 and n_col == 4 and bounds.shape[0] == 8:
        return wide_body(factor, rhs, parent, bounds, slot, structure, n_row, n_col)
    return general_body(factor, rhs, parent, bounds, slot, structure, n_row)


def solution(mesh):
    in_specs = (P("row", "col"), P("row", "col"), P(), P(), P(), P())
    out_specs = P("row", "col")
    step = functools.partial(body, n_row=mesh.shape["row"], n_col=mesh.shape["col"])
    return jax.shard_map(step, mesh=mesh, in_specs=in_specs, out_specs=out_specs, check_vma=False)
```

```python
import functools
import itertools

import jax
import jax.numpy as jnp
import numpy as np
from jax import lax
from jax.experimental import pallas as pl
from jax.experimental.pallas import tpu as pltpu
from jax.sharding import PartitionSpec as P

SMEM = pl.BlockSpec(memory_space=pltpu.SMEM)
VMEM = pl.BlockSpec(memory_space=pltpu.VMEM)
ANY = pl.BlockSpec(memory_space=pl.ANY)
HIGHEST = lax.Precision.HIGHEST
F32 = jnp.float32
BF16 = jnp.bfloat16
SMALL = pltpu.CompilerParams(vmem_limit_bytes=4 * 1024 * 1024)


def block_masks(parent, bounds, slot, structure):
    count = slot.shape[0]
    ar = jnp.arange(count, dtype=jnp.int32)
    logical = jnp.sum(jnp.where(slot[:, None] == ar[None, :], ar[:, None], 0), axis=0)
    node = jnp.sum((logical[:, None] >= bounds[None, 1:7]).astype(jnp.int32), axis=1)
    level = (node >= 4).astype(jnp.int32) + (node >= 6).astype(jnp.int32)
    nodes = jnp.arange(7, dtype=jnp.int32)
    grand = parent[parent]
    ancestor = ((nodes[None, :] == parent[:, None]) | (nodes[None, :] == grand[:, None])) & (
        nodes[None, :] != nodes[:, None]
    )
    node_hot = (node[:, None] == nodes[None, :]).astype(jnp.float32)
    perm_hot = (logical[:, None] == ar[None, :]).astype(jnp.float32)
    listed_store = jnp.dot(structure.astype(jnp.float32), perm_hot.T, precision=HIGHEST)
    anc_pairs = jnp.dot(
        node_hot, jnp.dot(ancestor.astype(jnp.float32), node_hot.T, precision=HIGHEST), precision=HIGHEST
    )
    list_pairs = jnp.dot(node_hot, listed_store, precision=HIGHEST)
    link = (anc_pairs * list_pairs).T > 0.5
    same = node[:, None] == node[None, :]
    return level, same, link


def masked(block_rows, mask):
    rblocks, width = mask.shape
    bsz = block_rows.shape[0] // rblocks
    shaped = block_rows.reshape(rblocks, bsz, width, bsz) * mask[:, None, :, None].astype(jnp.float32)
    return shaped.reshape(block_rows.shape)


def general_body(factor, rhs, parent, bounds, slot, structure, n_row):
    level, same, link = block_masks(parent, bounds, slot, structure)
    held = slot.shape[0] // n_row
    bsz = factor.shape[0] // held
    first = lax.axis_index("row") * held
    level_mine = lax.dynamic_slice_in_dim(level, first, held, 0)
    same_mine = lax.dynamic_slice_in_dim(same, first, held, 0)
    link_mine = lax.dynamic_slice_in_dim(link, first, held, 0)
    full_rows = lax.all_gather(factor, "col", axis=1, tiled=True)
    diag_part = masked(full_rows, same_mine)
    link_part = masked(full_rows, link_mine)

    def product(matrix, vector):
        return jnp.dot(
            matrix,
            lax.all_gather(vector, "row", axis=0, tiled=True),
            precision=HIGHEST,
            preferred_element_type=jnp.float32,
        )

    acc = jnp.zeros(rhs.shape, jnp.float32)
    result = jnp.zeros(rhs.shape, jnp.float32)
    for section in range(3):
        rows = jnp.repeat(level_mine == section, bsz)[:, None]
        solved = jnp.where(rows, product(diag_part, rhs - acc), 0.0)
        result = result + solved
        if section < 2:
            acc = acc + product(link_part, solved)
    return result


ON = 0
SAME = 3
PARTNER = 8
HEAD = 16
LINK0 = 0
LINK1 = 8
AT_ONE = 40
AT_TWO = 41
FACTS = 48

MASK_PAIRS = list(itertools.combinations(range(1, 8), 2))


def mask_table():
    table = np.zeros((8, 8), np.int32)
    for i, (u, v) in enumerate(MASK_PAIRS):
        table[u, v] = table[v, u] = i
    return table


def as_int(flag):
    return jnp.where(flag, jnp.int32(1), jnp.int32(0))


def fetch(pairs, sems):
    copies = [pltpu.make_async_copy(a, b, sems.at[i]) for i, (a, b) in enumerate(pairs)]
    for copy in copies:
        copy.start()
    for copy in copies:
        copy.wait()


def wide_block(bounds):
    wide = jnp.int32(0)
    for s in range(1, 7):
        wide = wide + as_int(bounds[s] == s)
    return wide


def level_of(node):
    return as_int(node >= 4) + as_int(node >= 6)


def set_row(masks, row, flag):
    masks[row : row + 1, :] = jnp.full((1, masks.shape[1]), as_int(flag).astype(F32))


def split_piece(j, piece, high, low):
    bsz = piece.shape[0]
    for h in range(2):
        high[2 * j + h], low[2 * j + h] = split(piece[:, h * bsz : (h + 1) * bsz])


def split_kernel(both, f1, f2, high, low, masks):
    split_piece(1, f1, high, low)
    split_piece(2, f2, high, low)
    bounds, slot = both.at[:8], both.at[8:]
    p = lax.axis_index("row")
    wide = wide_block(bounds)
    m = slot[wide] ^ slot[wide + 1]
    place = jnp.int32(0)
    for i in range(1, 8):
        place = place + i * as_int(slot[i] == p)
    node = place - as_int(place > wide)
    masks[...] = jnp.zeros(masks.shape, F32)
    for k in range(3):
        set_row(masks, ON + k, level_of(node) == k)
    set_row(masks, SAME, node == wide)
    for k in range(8):
        set_row(masks, PARTNER + k, (node == wide) & (place_of(m) == k))


def facts_kernel(after, parent_in, bounds_in, slot_in, structure_in, table_in, masks, middle, spread, end, parent, bounds, slot, structure, table, logical, node, sems):
    del after
    pairs = [(parent_in, parent), (bounds_in, bounds), (slot_in, slot), (structure_in, structure), (table_in, table)]
    fetch(pairs, sems)
    p = lax.axis_index("row")
    c = lax.axis_index("col")
    wide = wide_block(bounds)
    wide_level = level_of(wide)
    m = slot[wide] ^ slot[wide + 1]
    for i in range(8):
        q = slot[i]
        logical[q] = i
        node[q] = i - as_int(i > wide)
    mine = node[p]
    place = logical[p]

    def linked(q):
        below = node[q]
        up = parent[below]
        top = parent[up]
        above = ((mine == up) | (mine == top)) & (mine != below)
        return above & (structure[below, place] == 1)

    links = [(linked(k ^ (2 * c)), node[k ^ (2 * c)]) for k in range(8)]
    for k, (on, below) in enumerate(links):
        set_row(masks, LINK0 + k, on & (below < 4))
    top = slot[7]
    u = slot[jnp.where(wide_level == 2, 4, 5)] ^ top
    v = slot[jnp.where(wide_level == 2, 5, 6)] ^ top
    third = slot[4] ^ top

    def set_index(index, value):
        index[...] = jnp.full(index.shape, value)

    set_index(middle, jnp.where(wide_level == 1, m, 0))
    set_index(spread, table[u, v] + len(MASK_PAIRS) * as_int(wide_level == 1))
    set_index(end, jnp.where(wide_level == 1, third, jnp.where(wide_level == 2, 7 + m, 0)))
    low = jnp.minimum(u, v)
    high = jnp.maximum(u, v)
    at_two = wide_level == 2
    picks = [low, high, jnp.where(at_two, low ^ m, third), high ^ m]
    for s in range(4):
        fresh = [True, True, wide_level >= 1, at_two][s]
        for j in range(min(s, 2)):
            fresh = fresh & (picks[s] != picks[j])
        at = place_of(picks[s])
        for k, (on, below) in enumerate(links):
            set_row(masks, LINK1 + 8 * s + k, on & (below >= 4) & (below < 6) & fresh & (at == k))
    set_row(masks, AT_ONE, wide_level == 1)
    set_row(masks, AT_TWO, at_two)


def split(value):
    high = value.astype(BF16)
    return high, (value - high.astype(F32)).astype(BF16)


def dot(high, low, value):
    value_high, value_low = split(value)
    small = jnp.dot(high, value_low, preferred_element_type=F32) + jnp.dot(low, value_high, preferred_element_type=F32)
    return jnp.dot(high, value_high, preferred_element_type=F32) + small


def place_of(mask):
    return lax.axis_index("row") ^ mask ^ (2 * lax.axis_index("col"))


def row_of(masks, row):
    return masks[row : row + 1, :]


def own_part(head, high, low, level, mine):
    at = place_of(0)
    return dot(high[at], low[at], mine) * row_of(head, ON + level)


def partner_part(head, high, low, level, partner):
    on = row_of(head, SAME) * row_of(head, ON + level)
    block = [jnp.zeros(high.shape[1:], BF16) for _ in range(2)]
    for k in range(8):
        pick = row_of(head, PARTNER + k).astype(BF16)
        block = [block[0] + high[k] * pick, block[1] + low[k] * pick]
    return dot(block[0], block[1], jnp.where(on > 0, partner, 0.0))


def first_kernel(head, rhs, partner, f0, f3, high_in, low_in, y, high, low):
    del high_in, low_in
    split_piece(0, f0, high, low)
    split_piece(3, f3, high, low)
    y[...] = own_part(head, high, low, 0, rhs[...]) + partner_part(head, high, low, 0, partner[...])


def unread_kernel(*outs):
    del outs


def second_kernel(head, facts, rhs, high, low, *rest):
    ys, (t, y) = rest[:-2], rest[-2:]
    total = rhs[...]
    for k, block in enumerate(ys):
        at = place_of(k)
        total = total - dot(high[at], low[at], block[...] * facts[pl.ds(LINK0 + at, 1), :])
    t[...] = total
    y[...] = own_part(head, high, low, 1, total)


def partner_kernel(head, high, low, y_in, partner, y):
    y[...] = y_in[...] + partner_part(head, high, low, 1, partner[...])


def less_linked(facts, high, low, t, zs):
    total = t
    for k in range(8):
        value = jnp.zeros(t.shape, F32)
        for s, z in enumerate(zs):
            value = value + jnp.where(row_of(facts, LINK1 + 8 * s + k) > 0, z, 0.0)
        total = total - dot(high[k], low[k], value)
    return total


def wide_last_kernel(facts, high, low, t, z0, z1, z2, z3, total):
    total[...] = less_linked(facts, high, low, t[...], [z0[...], z1[...], z2[...], z3[...]])


def third_kernel(head, facts, high, low, t, y0, y1, fixed, z0, z1, extra, partner, out):
    at_two = row_of(facts, AT_TWO) > 0
    last = jnp.where(at_two, extra[...], less_linked(facts, high, low, t[...], [z0[...], z1[...], extra[...]]))
    y2 = own_part(head, high, low, 2, last) + partner_part(head, high, low, 2, partner[...])
    out[...] = y0[...] + jnp.where(row_of(facts, AT_ONE) > 0, fixed[...], y1[...]) + y2


def call(kernel, args, outs, n_smem=0, aliases=()):
    outs = [jax.ShapeDtypeStruct(*o) if isinstance(o[0], tuple) else jax.ShapeDtypeStruct(o, F32) for o in outs]
    return pl.pallas_call(
        kernel,
        in_specs=[SMEM] * n_smem + [VMEM] * (len(args) - n_smem),
        out_specs=[VMEM] * len(outs),
        out_shape=outs,
        input_output_aliases=dict(aliases),
        compiler_params=SMALL,
    )(*args)


def unread(shape, count):
    outs = [jax.ShapeDtypeStruct(shape, F32)] * count
    return pl.pallas_call(unread_kernel, out_specs=[ANY] * count, out_shape=outs, compiler_params=SMALL)()


def find_facts(after, parent, bounds, slot, structure, table):
    i32 = jnp.int32
    args = [parent, bounds, slot, structure, jnp.asarray(table)]
    index = jax.ShapeDtypeStruct((128,), i32)
    return pl.pallas_call(
        facts_kernel,
        in_specs=[ANY] * 6,
        out_specs=[VMEM] * 4,
        out_shape=[jax.ShapeDtypeStruct((FACTS, 128), F32), index, index, index],
        scratch_shapes=[pltpu.SMEM(a.shape, i32) for a in args]
        + [pltpu.SMEM((8,), i32), pltpu.SMEM((8,), i32), pltpu.SemaphoreType.DMA((5,))],
        compiler_params=SMALL,
    )(after, *args)


def first_switch(bounds, slot):
    i = jnp.arange(4, dtype=jnp.int32)
    wide = (bounds[:4] == i) & (bounds[1:5] == i + 2)
    return jnp.sum(jnp.where(wide, slot[:4] ^ slot[1:5], 0))


def wide_body(factor, rhs, parent, bounds, slot, structure, n_row, n_col):
    bsz, cols = rhs.shape
    block = (bsz, cols)

    def send(value, row_mask, col_mask=0):
        pairs = [
            (r * n_col + k, (r ^ row_mask) * n_col + (k ^ col_mask)) for r in range(n_row) for k in range(n_col)
        ]
        return lax.ppermute(value, ("row", "col"), pairs)

    first = first_switch(bounds, slot)
    factor, rhs, first = lax.optimization_barrier((factor, rhs, first))
    f0 = factor
    f2 = send(f0, 0, 2)
    f1 = send(f0, 0, 1)
    def exchange(mask, value):
        return send(value, mask) if mask else unread(block, 1)[0]

    partner = lax.switch(first, [functools.partial(exchange, k) for k in range(n_row)], rhs)
    f2, partner = lax.optimization_barrier((f2, partner))
    f3 = send(f2, 0, 1)
    parts = ((n_row, bsz, bsz), BF16)
    both = jnp.concatenate([bounds, slot])
    high, low, head = call(split_kernel, [both, f1, f2], [parts, parts, (HEAD, cols)], 1)
    y0, high, low = call(
        first_kernel, [head, rhs, partner, f0, f3, high, low], [block, parts, parts], aliases={5: 1, 6: 2}
    )

    far = send(y0, 4)
    near = [send(y0, k) for k in (1, 2, 3)]
    ys = [y0] + near + [far] + [send(far, k) for k in (1, 2, 3)]
    facts, at_middle, at_spread, at_end = find_facts(near[0], parent, bounds, slot, structure, mask_table())
    t, y1 = call(second_kernel, [head, facts, rhs, high, low] + ys, [block, block])

    def middle(mask, head, high, low, t, y1):
        if not mask:
            return unread(block, 1)[0]
        return call(partner_kernel, [head, high, low, y1, send(t, mask)], [block])[0]

    fixed = lax.switch(
        at_middle[0], [functools.partial(middle, k) for k in range(n_row)], head, high, low, t, y1
    )

    z0, z1 = lax.switch(
        at_spread[0],
        [lambda y, fixed, u=u, v=v: (send(y, u), send(y, v)) for u, v in MASK_PAIRS]
        + [lambda y, fixed, u=u, v=v: (send(fixed, u), send(fixed, v)) for u, v in MASK_PAIRS],
        y1,
        fixed,
    )

    def end(mask, level, facts, high, low, t, fixed, z0, z1):
        if not mask:
            return tuple(unread(block, 2))
        if level == 1:
            return send(fixed, mask), *unread(block, 1)
        (wide_t,) = call(wide_last_kernel, [facts, high, low, t, z0, z1, send(z0, mask), send(z1, mask)], [block])
        return wide_t, send(wide_t, mask)

    extra, partner = lax.switch(
        at_end[0],
        [functools.partial(end, k, 1) for k in range(n_row)] + [functools.partial(end, k, 2) for k in range(1, n_row)],
        *(facts, high, low, t, fixed, z0, z1),
    )
    args = [head, facts, high, low, t, y0, y1, fixed, z0, z1, extra, partner]
    return call(third_kernel, args, [block])[0]


def body(factor, rhs, parent, bounds, slot, structure, n_row, n_col):
    count = slot.shape[0]
    if count == 8 and n_row == 8 and n_col == 4 and bounds.shape[0] == 8:
        return wide_body(factor, rhs, parent, bounds, slot, structure, n_row, n_col)
    return general_body(factor, rhs, parent, bounds, slot, structure, n_row)


def solution(mesh):
    in_specs = (P("row", "col"), P("row", "col"), P(), P(), P(), P())
    out_specs = P("row", "col")
    step = functools.partial(body, n_row=mesh.shape["row"], n_col=mesh.shape["col"])
    return jax.shard_map(step, mesh=mesh, in_specs=in_specs, out_specs=out_specs, check_vma=False)
```

```python
import functools
import itertools
import operator

import jax
import jax.numpy as jnp
import numpy as np
from jax import lax
from jax.experimental import pallas as pl
from jax.experimental.pallas import tpu as pltpu
from jax.sharding import PartitionSpec as P

SMEM = pl.BlockSpec(memory_space=pltpu.SMEM)
VMEM = pl.BlockSpec(memory_space=pltpu.VMEM)
ANY = pl.BlockSpec(memory_space=pl.ANY)
HIGHEST = lax.Precision.HIGHEST
F32 = jnp.float32
BF16 = jnp.bfloat16
SMALL = pltpu.CompilerParams(vmem_limit_bytes=4 * 1024 * 1024)


def block_masks(parent, bounds, slot, structure):
    count = slot.shape[0]
    ar = jnp.arange(count, dtype=jnp.int32)
    logical = jnp.sum(jnp.where(slot[:, None] == ar[None, :], ar[:, None], 0), axis=0)
    node = jnp.sum((logical[:, None] >= bounds[None, 1:7]).astype(jnp.int32), axis=1)
    level = (node >= 4).astype(jnp.int32) + (node >= 6).astype(jnp.int32)
    nodes = jnp.arange(7, dtype=jnp.int32)
    grand = parent[parent]
    ancestor = ((nodes[None, :] == parent[:, None]) | (nodes[None, :] == grand[:, None])) & (
        nodes[None, :] != nodes[:, None]
    )
    node_hot = (node[:, None] == nodes[None, :]).astype(jnp.float32)
    perm_hot = (logical[:, None] == ar[None, :]).astype(jnp.float32)
    listed_store = jnp.dot(structure.astype(jnp.float32), perm_hot.T, precision=HIGHEST)
    anc_pairs = jnp.dot(
        node_hot, jnp.dot(ancestor.astype(jnp.float32), node_hot.T, precision=HIGHEST), precision=HIGHEST
    )
    list_pairs = jnp.dot(node_hot, listed_store, precision=HIGHEST)
    link = (anc_pairs * list_pairs).T > 0.5
    same = node[:, None] == node[None, :]
    return level, same, link


def masked(block_rows, mask):
    rblocks, width = mask.shape
    bsz = block_rows.shape[0] // rblocks
    shaped = block_rows.reshape(rblocks, bsz, width, bsz) * mask[:, None, :, None].astype(jnp.float32)
    return shaped.reshape(block_rows.shape)


def general_body(factor, rhs, parent, bounds, slot, structure, n_row):
    level, same, link = block_masks(parent, bounds, slot, structure)
    held = slot.shape[0] // n_row
    bsz = factor.shape[0] // held
    first = lax.axis_index("row") * held
    level_mine = lax.dynamic_slice_in_dim(level, first, held, 0)
    same_mine = lax.dynamic_slice_in_dim(same, first, held, 0)
    link_mine = lax.dynamic_slice_in_dim(link, first, held, 0)
    full_rows = lax.all_gather(factor, "col", axis=1, tiled=True)
    diag_part = masked(full_rows, same_mine)
    link_part = masked(full_rows, link_mine)

    def product(matrix, vector):
        return jnp.dot(
            matrix,
            lax.all_gather(vector, "row", axis=0, tiled=True),
            precision=HIGHEST,
            preferred_element_type=jnp.float32,
        )

    acc = jnp.zeros(rhs.shape, jnp.float32)
    result = jnp.zeros(rhs.shape, jnp.float32)
    for section in range(3):
        rows = jnp.repeat(level_mine == section, bsz)[:, None]
        solved = jnp.where(rows, product(diag_part, rhs - acc), 0.0)
        result = result + solved
        if section < 2:
            acc = acc + product(link_part, solved)
    return result


ON = 0
SAME = 3
PARTNER = 8
HEAD = 16
LINK0 = 0
LINK1 = 8
AT_ONE = 40
AT_TWO = 41
FACTS = 48

MASK_PAIRS = list(itertools.combinations(range(1, 8), 2))
MASK_SETS = [
    s for size in (3, 4) for s in itertools.combinations(range(1, 8), size) if functools.reduce(operator.xor, s) == 0
]


def mask_table():
    table = np.zeros(256, np.int32)
    for i, masks in enumerate(MASK_PAIRS + MASK_SETS):
        table[sum(1 << k for k in masks)] = i
    return table


def as_int(flag):
    return jnp.where(flag, jnp.int32(1), jnp.int32(0))


def fetch(pairs, sems):
    copies = [pltpu.make_async_copy(a, b, sems.at[i]) for i, (a, b) in enumerate(pairs)]
    for copy in copies:
        copy.start()
    for copy in copies:
        copy.wait()


def wide_block(bounds):
    wide = jnp.int32(0)
    for s in range(1, 7):
        wide = wide + as_int(bounds[s] == s)
    return wide


def level_of(node):
    return as_int(node >= 4) + as_int(node >= 6)


def set_row(masks, row, flag):
    masks[row : row + 1, :] = jnp.full((1, masks.shape[1]), as_int(flag).astype(F32))


def split_piece(j, piece, high, low):
    bsz = piece.shape[0]
    for h in range(2):
        high[2 * j + h], low[2 * j + h] = split(piece[:, h * bsz : (h + 1) * bsz])


def split_kernel(both, f1, f2, high, low, masks):
    split_piece(1, f1, high, low)
    split_piece(2, f2, high, low)
    bounds, slot = both.at[:8], both.at[8:]
    p = lax.axis_index("row")
    wide = wide_block(bounds)
    m = slot[wide] ^ slot[wide + 1]
    place = jnp.int32(0)
    for i in range(1, 8):
        place = place + i * as_int(slot[i] == p)
    node = place - as_int(place > wide)
    masks[...] = jnp.zeros(masks.shape, F32)
    for k in range(3):
        set_row(masks, ON + k, level_of(node) == k)
    set_row(masks, SAME, node == wide)
    for k in range(8):
        set_row(masks, PARTNER + k, (node == wide) & (place_of(m) == k))


def facts_kernel(after, parent_in, bounds_in, slot_in, structure_in, table_in, masks, middle, spread, end, parent, bounds, slot, structure, table, logical, node, link1, sems):
    del after
    pairs = [(parent_in, parent), (bounds_in, bounds), (slot_in, slot), (structure_in, structure), (table_in, table)]
    fetch(pairs, sems)
    p = lax.axis_index("row")
    c = lax.axis_index("col")
    wide = wide_block(bounds)
    wide_level = level_of(wide)
    m = slot[wide] ^ slot[wide + 1]
    for i in range(8):
        q = slot[i]
        logical[q] = i
        node[q] = i - as_int(i > wide)
    mine = node[p]
    place = logical[p]

    def linked(q):
        below = node[q]
        up = parent[below]
        top = parent[up]
        above = ((mine == up) | (mine == top)) & (mine != below)
        return above & (structure[below, place] == 1)

    masks[...] = jnp.zeros(masks.shape, F32)
    for k in range(8):
        q = k ^ (2 * c)
        on = linked(q)
        set_row(masks, LINK0 + k, on & (node[q] < 4))
        link1[k] = as_int(on & (node[q] >= 4) & (node[q] < 6))
    at_one = wide_level == 1
    at_two = wide_level == 2
    top = slot[7]
    u = slot[jnp.where(at_two, 4, 5)] ^ top
    v = slot[jnp.where(at_two, 5, 6)] ^ top
    third = slot[4] ^ top
    fourth = u ^ v ^ third
    one = jnp.int32(1)
    bits = (one << u) | (one << v)
    bits = bits | jnp.where(at_one, (one << third) | ((one << fourth) & 254), 0)
    bits = bits | jnp.where(at_two, (one << (u ^ m)) | (one << (v ^ m)), 0)

    def set_index(index, value):
        index[...] = jnp.full(index.shape, value)

    set_index(middle, jnp.where(at_one, m, jnp.where(at_two, 8, 0)))
    set_index(spread, table[bits])
    set_index(end, jnp.where(at_two, m, 0))

    def set_link(s, mask, on):
        at = place_of(mask)

        @pl.when(on)
        def _():
            row = LINK1 + 8 * s + at
            masks[pl.ds(row, 1), :] = jnp.full((1, masks.shape[1]), link1[at].astype(F32))

    count = jnp.int32(0)
    for k in range(1, 8):
        on = (bits >> k) & 1
        set_link(count, k, on == 1)
        count = count + on
    set_row(masks, AT_ONE, at_one)
    set_row(masks, AT_TWO, at_two)


def split(value):
    high = value.astype(BF16)
    return high, (value - high.astype(F32)).astype(BF16)


def dot(high, low, value):
    value_high, value_low = split(value)
    small = jnp.dot(high, value_low, preferred_element_type=F32) + jnp.dot(low, value_high, preferred_element_type=F32)
    return jnp.dot(high, value_high, preferred_element_type=F32) + small


def place_of(mask):
    return lax.axis_index("row") ^ mask ^ (2 * lax.axis_index("col"))


def row_of(masks, row):
    return masks[row : row + 1, :]


def own_part(head, high, low, level, mine):
    at = place_of(0)
    return dot(high[at], low[at], mine) * row_of(head, ON + level)


def partner_part(head, high, low, level, partner):
    on = row_of(head, SAME) * row_of(head, ON + level)
    block = [jnp.zeros(high.shape[1:], BF16) for _ in range(2)]
    for k in range(8):
        pick = row_of(head, PARTNER + k).astype(BF16)
        block = [block[0] + high[k] * pick, block[1] + low[k] * pick]
    return dot(block[0], block[1], jnp.where(on > 0, partner, 0.0))


def first_kernel(head, rhs, partner, f0, f3, high_in, low_in, y, high, low):
    del high_in, low_in
    split_piece(0, f0, high, low)
    split_piece(3, f3, high, low)
    y[...] = own_part(head, high, low, 0, rhs[...]) + partner_part(head, high, low, 0, partner[...])


def unread_kernel(*outs):
    del outs


def second_kernel(head, facts, rhs, high, low, *rest):
    ys, (t, y) = rest[:-2], rest[-2:]
    total = rhs[...]
    for k, block in enumerate(ys):
        at = place_of(k)
        total = total - dot(high[at], low[at], block[...] * facts[pl.ds(LINK0 + at, 1), :])
    t[...] = total
    y[...] = own_part(head, high, low, 1, total)


def partner_kernel(head, high, low, y_in, partner, y):
    y[...] = y_in[...] + partner_part(head, high, low, 1, partner[...])


def copy_kernel(y_in, y):
    y[...] = y_in[...]


def less_linked(facts, high, low, t, zs):
    total = t
    for k in range(8):
        value = jnp.zeros(t.shape, F32)
        for s, z in enumerate(zs):
            value = value + jnp.where(row_of(facts, LINK1 + 8 * s + k) > 0, z, 0.0)
        total = total - dot(high[k], low[k], value)
    return total


def wide_last_kernel(facts, high, low, t, z0, z1, z2, z3, total):
    total[...] = less_linked(facts, high, low, t[...], [z0[...], z1[...], z2[...], z3[...]])


def third_kernel(head, facts, high, low, t, y0, y1, fixed, z0, z1, z2, z3, wide_t, partner, out):
    at_two = row_of(facts, AT_TWO) > 0
    last = jnp.where(at_two, wide_t[...], less_linked(facts, high, low, t[...], [z0[...], z1[...], z2[...], z3[...]]))
    y2 = own_part(head, high, low, 2, last) + partner_part(head, high, low, 2, partner[...])
    out[...] = y0[...] + jnp.where(row_of(facts, AT_ONE) > 0, fixed[...], y1[...]) + y2


def call(kernel, args, outs, n_smem=0, aliases=()):
    outs = [jax.ShapeDtypeStruct(*o) if isinstance(o[0], tuple) else jax.ShapeDtypeStruct(o, F32) for o in outs]
    return pl.pallas_call(
        kernel,
        in_specs=[SMEM] * n_smem + [VMEM] * (len(args) - n_smem),
        out_specs=[VMEM] * len(outs),
        out_shape=outs,
        input_output_aliases=dict(aliases),
        compiler_params=SMALL,
    )(*args)


def unread(shape, count):
    if not count:
        return ()
    outs = [jax.ShapeDtypeStruct(shape, F32)] * count
    return pl.pallas_call(unread_kernel, out_specs=[ANY] * count, out_shape=outs, compiler_params=SMALL)()


def find_facts(after, parent, bounds, slot, structure, table):
    i32 = jnp.int32
    args = [parent, bounds, slot, structure, jnp.asarray(table)]
    index = jax.ShapeDtypeStruct((128,), i32)
    return pl.pallas_call(
        facts_kernel,
        in_specs=[ANY] * 6,
        out_specs=[VMEM] * 4,
        out_shape=[jax.ShapeDtypeStruct((FACTS, 128), F32), index, index, index],
        scratch_shapes=[pltpu.SMEM(a.shape, i32) for a in args]
        + [pltpu.SMEM((8,), i32)] * 3
        + [pltpu.SemaphoreType.DMA((5,))],
        compiler_params=SMALL,
    )(after, *args)


def first_switch(bounds, slot):
    i = jnp.arange(4, dtype=jnp.int32)
    wide = (bounds[:4] == i) & (bounds[1:5] == i + 2)
    return jnp.sum(jnp.where(wide, slot[:4] ^ slot[1:5], 0))


def wide_body(factor, rhs, parent, bounds, slot, structure, n_row, n_col):
    bsz, cols = rhs.shape
    block = (bsz, cols)

    def send(value, row_mask, col_mask=0):
        pairs = [
            (r * n_col + k, (r ^ row_mask) * n_col + (k ^ col_mask)) for r in range(n_row) for k in range(n_col)
        ]
        return lax.ppermute(value, ("row", "col"), pairs)

    first = first_switch(bounds, slot)
    factor, rhs, first = lax.optimization_barrier((factor, rhs, first))
    f0 = factor
    f2 = send(f0, 0, 2)
    f1 = send(f0, 0, 1)
    def exchange(mask, value):
        return send(value, mask) if mask else unread(block, 1)[0]

    partner = lax.switch(first, [functools.partial(exchange, k) for k in range(n_row)], rhs)
    f2, partner = lax.optimization_barrier((f2, partner))
    f3 = send(f2, 0, 1)
    parts = ((n_row, bsz, bsz), BF16)
    both = jnp.concatenate([bounds, slot])
    high, low, head = call(split_kernel, [both, f1, f2], [parts, parts, (HEAD, cols)], 1)
    y0, high, low = call(
        first_kernel, [head, rhs, partner, f0, f3, high, low], [block, parts, parts], aliases={5: 1, 6: 2}
    )

    far = send(y0, 4)
    near = [send(y0, k) for k in (1, 2, 3)]
    ys = [y0] + near + [far] + [send(far, k) for k in (1, 2, 3)]
    facts, at_middle, at_spread, at_end = find_facts(near[0], parent, bounds, slot, structure, mask_table())
    t, y1 = call(second_kernel, [head, facts, rhs, high, low] + ys, [block, block])

    def middle(mask, head, high, low, t, y1):
        if not mask:
            return unread(block, 1)[0]
        if mask == n_row:
            return call(copy_kernel, [y1], [block])[0]
        return call(partner_kernel, [head, high, low, y1, send(t, mask)], [block])[0]

    fixed = lax.switch(
        at_middle[0], [functools.partial(middle, k) for k in range(n_row + 1)], head, high, low, t, y1
    )

    def spread(masks, y, fixed):
        blocks = [send(y if masks in MASK_PAIRS else fixed, k) for k in masks]
        return tuple(blocks + list(unread(block, 4 - len(masks))))

    zs = lax.switch(at_spread[0], [functools.partial(spread, masks) for masks in MASK_PAIRS + MASK_SETS], y1, fixed)
    def end(mask, facts, high, low, t, *zs):
        if not mask:
            return tuple(unread(block, 2))
        (wide_t,) = call(wide_last_kernel, [facts, high, low, t, *zs], [block])
        return wide_t, send(wide_t, mask)

    wide_t, partner = lax.switch(
        at_end[0], [functools.partial(end, k) for k in range(n_row)], facts, high, low, t, *zs
    )
    args = [head, facts, high, low, t, y0, y1, fixed, *zs, wide_t, partner]
    return call(third_kernel, args, [block])[0]


def body(factor, rhs, parent, bounds, slot, structure, n_row, n_col):
    count = slot.shape[0]
    if count == 8 and n_row == 8 and n_col == 4 and bounds.shape[0] == 8:
        return wide_body(factor, rhs, parent, bounds, slot, structure, n_row, n_col)
    return general_body(factor, rhs, parent, bounds, slot, structure, n_row)


def solution(mesh):
    in_specs = (P("row", "col"), P("row", "col"), P(), P(), P(), P())
    out_specs = P("row", "col")
    step = functools.partial(body, n_row=mesh.shape["row"], n_col=mesh.shape["col"])
    return jax.shard_map(step, mesh=mesh, in_specs=in_specs, out_specs=out_specs, check_vma=False)
```

```python
import functools
import itertools
import operator

import jax
import jax.numpy as jnp
import numpy as np
from jax import lax
from jax.experimental import pallas as pl
from jax.experimental.pallas import tpu as pltpu
from jax.sharding import PartitionSpec as P

SMEM = pl.BlockSpec(memory_space=pltpu.SMEM)
VMEM = pl.BlockSpec(memory_space=pltpu.VMEM)
ANY = pl.BlockSpec(memory_space=pl.ANY)
HIGHEST = lax.Precision.HIGHEST
F32 = jnp.float32
BF16 = jnp.bfloat16
SMALL = pltpu.CompilerParams(vmem_limit_bytes=4 * 1024 * 1024)


def block_masks(parent, bounds, slot, structure):
    count = slot.shape[0]
    ar = jnp.arange(count, dtype=jnp.int32)
    logical = jnp.sum(jnp.where(slot[:, None] == ar[None, :], ar[:, None], 0), axis=0)
    node = jnp.sum((logical[:, None] >= bounds[None, 1:7]).astype(jnp.int32), axis=1)
    level = (node >= 4).astype(jnp.int32) + (node >= 6).astype(jnp.int32)
    nodes = jnp.arange(7, dtype=jnp.int32)
    grand = parent[parent]
    ancestor = ((nodes[None, :] == parent[:, None]) | (nodes[None, :] == grand[:, None])) & (
        nodes[None, :] != nodes[:, None]
    )
    node_hot = (node[:, None] == nodes[None, :]).astype(jnp.float32)
    perm_hot = (logical[:, None] == ar[None, :]).astype(jnp.float32)
    listed_store = jnp.dot(structure.astype(jnp.float32), perm_hot.T, precision=HIGHEST)
    anc_pairs = jnp.dot(
        node_hot, jnp.dot(ancestor.astype(jnp.float32), node_hot.T, precision=HIGHEST), precision=HIGHEST
    )
    list_pairs = jnp.dot(node_hot, listed_store, precision=HIGHEST)
    link = (anc_pairs * list_pairs).T > 0.5
    same = node[:, None] == node[None, :]
    return level, same, link


def masked(block_rows, mask):
    rblocks, width = mask.shape
    bsz = block_rows.shape[0] // rblocks
    shaped = block_rows.reshape(rblocks, bsz, width, bsz) * mask[:, None, :, None].astype(jnp.float32)
    return shaped.reshape(block_rows.shape)


def general_body(factor, rhs, parent, bounds, slot, structure, n_row):
    level, same, link = block_masks(parent, bounds, slot, structure)
    held = slot.shape[0] // n_row
    bsz = factor.shape[0] // held
    first = lax.axis_index("row") * held
    level_mine = lax.dynamic_slice_in_dim(level, first, held, 0)
    same_mine = lax.dynamic_slice_in_dim(same, first, held, 0)
    link_mine = lax.dynamic_slice_in_dim(link, first, held, 0)
    full_rows = lax.all_gather(factor, "col", axis=1, tiled=True)
    diag_part = masked(full_rows, same_mine)
    link_part = masked(full_rows, link_mine)

    def product(matrix, vector):
        return jnp.dot(
            matrix,
            lax.all_gather(vector, "row", axis=0, tiled=True),
            precision=HIGHEST,
            preferred_element_type=jnp.float32,
        )

    acc = jnp.zeros(rhs.shape, jnp.float32)
    result = jnp.zeros(rhs.shape, jnp.float32)
    for section in range(3):
        rows = jnp.repeat(level_mine == section, bsz)[:, None]
        solved = jnp.where(rows, product(diag_part, rhs - acc), 0.0)
        result = result + solved
        if section < 2:
            acc = acc + product(link_part, solved)
    return result


ON = 0
SAME = 3
PARTNER = 8
HEAD = 16
LINK0 = 0
LINK1 = 8
FACTS = 40

MASK_PAIRS = list(itertools.combinations(range(1, 8), 2))
MASK_SETS = [
    s for size in (3, 4) for s in itertools.combinations(range(1, 8), size) if functools.reduce(operator.xor, s) == 0
]


def mask_table():
    table = np.zeros(256, np.int32)
    for i, masks in enumerate(MASK_PAIRS + MASK_SETS):
        table[sum(1 << k for k in masks)] = i
    return table


def as_int(flag):
    return jnp.where(flag, jnp.int32(1), jnp.int32(0))


def fetch(pairs, sems):
    copies = [pltpu.make_async_copy(a, b, sems.at[i]) for i, (a, b) in enumerate(pairs)]
    for copy in copies:
        copy.start()
    for copy in copies:
        copy.wait()


def wide_block(bounds):
    wide = jnp.int32(0)
    for s in range(1, 7):
        wide = wide + as_int(bounds[s] == s)
    return wide


def level_of(node):
    return as_int(node >= 4) + as_int(node >= 6)


def set_row(masks, row, flag):
    masks[row : row + 1, :] = jnp.full((1, masks.shape[1]), as_int(flag).astype(F32))


def split_piece(j, piece, high, low):
    bsz = piece.shape[0]
    for h in range(2):
        high[2 * j + h], low[2 * j + h] = split(piece[:, h * bsz : (h + 1) * bsz])


def split_kernel(bounds, slot, f1, f2, high, low, masks):
    split_piece(1, f1, high, low)
    split_piece(2, f2, high, low)
    p = lax.axis_index("row")
    wide = wide_block(bounds)
    m = slot[wide] ^ slot[wide + 1]
    place = jnp.int32(0)
    for i in range(1, 8):
        place = place + i * as_int(slot[i] == p)
    node = place - as_int(place > wide)
    masks[...] = jnp.zeros(masks.shape, F32)
    for k in range(3):
        set_row(masks, ON + k, level_of(node) == k)
    set_row(masks, SAME, node == wide)
    for k in range(8):
        set_row(masks, PARTNER + k, (node == wide) & (place_of(m) == k))


def facts_kernel(after, parent_in, bounds_in, slot_in, structure_in, table_in, masks, middle, spread, end, parent, bounds, slot, structure, table, logical, node, link1, sems):
    del after
    pairs = [(parent_in, parent), (bounds_in, bounds), (slot_in, slot), (structure_in, structure), (table_in, table)]
    fetch(pairs, sems)
    p = lax.axis_index("row")
    c = lax.axis_index("col")
    wide = wide_block(bounds)
    wide_level = level_of(wide)
    m = slot[wide] ^ slot[wide + 1]
    for i in range(8):
        q = slot[i]
        logical[q] = i
        node[q] = i - as_int(i > wide)
    mine = node[p]
    place = logical[p]

    def linked(q):
        below = node[q]
        up = parent[below]
        top = parent[up]
        above = ((mine == up) | (mine == top)) & (mine != below)
        return above & (structure[below, place] == 1)

    masks[...] = jnp.zeros(masks.shape, F32)
    for k in range(8):
        q = k ^ (2 * c)
        on = linked(q)
        set_row(masks, LINK0 + k, on & (node[q] < 4))
        link1[k] = as_int(on & (node[q] >= 4) & (node[q] < 6))
    at_one = wide_level == 1
    at_two = wide_level == 2
    top = slot[7]
    u = slot[jnp.where(at_two, 4, 5)] ^ top
    v = slot[jnp.where(at_two, 5, 6)] ^ top
    third = slot[4] ^ top
    fourth = u ^ v ^ third
    one = jnp.int32(1)
    bits = (one << u) | (one << v)
    bits = bits | jnp.where(at_one, (one << third) | ((one << fourth) & 254), 0)
    bits = bits | jnp.where(at_two, (one << (u ^ m)) | (one << (v ^ m)), 0)

    def set_index(index, value):
        index[...] = jnp.full(index.shape, value)

    set_index(middle, jnp.where(at_one, m, jnp.where(at_two, 8, 0)))
    set_index(spread, table[bits])
    set_index(end, jnp.where(at_one, 1, jnp.where(at_two, 1 + m, 0)))

    def set_link(s, mask, on):
        at = place_of(mask)

        @pl.when(on)
        def _():
            row = LINK1 + 8 * s + at
            masks[pl.ds(row, 1), :] = jnp.full((1, masks.shape[1]), link1[at].astype(F32))

    count = jnp.int32(0)
    for k in range(1, 8):
        on = (bits >> k) & 1
        set_link(count, k, on == 1)
        count = count + on


def split(value):
    high = value.astype(BF16)
    return high, (value - high.astype(F32)).astype(BF16)


def dot(high, low, value):
    value_high, value_low = split(value)
    small = jnp.dot(high, value_low, preferred_element_type=F32) + jnp.dot(low, value_high, preferred_element_type=F32)
    return jnp.dot(high, value_high, preferred_element_type=F32) + small


def place_of(mask):
    return lax.axis_index("row") ^ mask ^ (2 * lax.axis_index("col"))


def row_of(masks, row):
    return masks[row : row + 1, :]


def own_part(head, high, low, level, mine):
    at = place_of(0)
    return dot(high[at], low[at], mine) * row_of(head, ON + level)


def partner_part(head, high, low, level, partner):
    on = row_of(head, SAME) * row_of(head, ON + level)
    block = [jnp.zeros(high.shape[1:], BF16) for _ in range(2)]
    for k in range(8):
        pick = row_of(head, PARTNER + k).astype(BF16)
        block = [block[0] + high[k] * pick, block[1] + low[k] * pick]
    return dot(block[0], block[1], jnp.where(on > 0, partner, 0.0))


def first_kernel(head, rhs, partner, f0, f3, high_in, low_in, y, high, low):
    del high_in, low_in
    split_piece(0, f0, high, low)
    split_piece(3, f3, high, low)
    y[...] = own_part(head, high, low, 0, rhs[...]) + partner_part(head, high, low, 0, partner[...])


def unread_kernel(*outs):
    del outs


def second_kernel(head, facts, rhs, high, low, *rest):
    ys, (t, y) = rest[:-2], rest[-2:]
    total = rhs[...]
    for k, block in enumerate(ys):
        at = place_of(k)
        total = total - dot(high[at], low[at], block[...] * facts[pl.ds(LINK0 + at, 1), :])
    t[...] = total
    y[...] = own_part(head, high, low, 1, total)


def partner_kernel(head, high, low, y_in, partner, y):
    y[...] = y_in[...] + partner_part(head, high, low, 1, partner[...])


def keep_kernel(*refs):
    half = len(refs) // 2
    for given, kept in zip(refs[:half], refs[half:]):
        kept[...] = given[...]


def less_linked(facts, high, low, t, zs):
    total = t
    for k in range(8):
        value = jnp.zeros(t.shape, F32)
        for s, z in enumerate(zs):
            value = value + jnp.where(row_of(facts, LINK1 + 8 * s + k) > 0, z, 0.0)
        total = total - dot(high[k], low[k], value)
    return total


def residual_kernel(facts, high, low, t, z0, z1, z2, z3, total):
    total[...] = less_linked(facts, high, low, t[...], [z0[...], z1[...], z2[...], z3[...]])


def last_kernel(head, high, low, y0, y1, total, partner, out):
    y2 = own_part(head, high, low, 2, total[...]) + partner_part(head, high, low, 2, partner[...])
    out[...] = y0[...] + y1[...] + y2


def third_kernel(head, facts, high, low, t, y0, y1, *rest):
    zs, out = rest[:-1], rest[-1]
    total = less_linked(facts, high, low, t[...], [z[...] for z in zs])
    out[...] = y0[...] + y1[...] + own_part(head, high, low, 2, total)


def call(kernel, args, outs, n_smem=0, aliases=()):
    outs = [jax.ShapeDtypeStruct(*o) if isinstance(o[0], tuple) else jax.ShapeDtypeStruct(o, F32) for o in outs]
    return pl.pallas_call(
        kernel,
        in_specs=[SMEM] * n_smem + [VMEM] * (len(args) - n_smem),
        out_specs=[VMEM] * len(outs),
        out_shape=outs,
        input_output_aliases=dict(aliases),
        compiler_params=SMALL,
    )(*args)


def keep(blocks):
    return call(keep_kernel, blocks, [b.shape for b in blocks])


def unread(shape, count):
    if not count:
        return ()
    outs = [jax.ShapeDtypeStruct(shape, F32)] * count
    return pl.pallas_call(unread_kernel, out_specs=[ANY] * count, out_shape=outs, compiler_params=SMALL)()


def find_facts(after, parent, bounds, slot, structure, table):
    i32 = jnp.int32
    args = [parent, bounds, slot, structure, jnp.asarray(table)]
    index = jax.ShapeDtypeStruct((128,), i32)
    return pl.pallas_call(
        facts_kernel,
        in_specs=[ANY] * 6,
        out_specs=[VMEM] * 4,
        out_shape=[jax.ShapeDtypeStruct((FACTS, 128), F32), index, index, index],
        scratch_shapes=[pltpu.SMEM(a.shape, i32) for a in args]
        + [pltpu.SMEM((8,), i32)] * 3
        + [pltpu.SemaphoreType.DMA((5,))],
        compiler_params=SMALL,
    )(after, *args)


def first_switch(bounds, slot):
    i = jnp.arange(4, dtype=jnp.int32)
    wide = (bounds[:4] == i) & (bounds[1:5] == i + 2)
    return jnp.sum(jnp.where(wide, slot[:4] ^ slot[1:5], 0))


def wide_body(factor, rhs, parent, bounds, slot, structure, n_row, n_col):
    bsz, cols = rhs.shape
    block = (bsz, cols)

    def send(value, row_mask, col_mask=0):
        pairs = [
            (r * n_col + k, (r ^ row_mask) * n_col + (k ^ col_mask)) for r in range(n_row) for k in range(n_col)
        ]
        return lax.ppermute(value, ("row", "col"), pairs)

    first = first_switch(bounds, slot)
    factor, rhs, first = lax.optimization_barrier((factor, rhs, first))
    f0 = factor
    f2 = send(f0, 0, 2)
    f1 = send(f0, 0, 1)
    def exchange(mask, value):
        return keep([send(value, mask)])[0] if mask else unread(block, 1)[0]

    partner = lax.switch(first, [functools.partial(exchange, k) for k in range(n_row)], rhs)
    f2, partner = lax.optimization_barrier((f2, partner))
    f3 = send(f2, 0, 1)
    parts = ((n_row, bsz, bsz), BF16)
    high, low, head = call(split_kernel, [bounds, slot, f1, f2], [parts, parts, (HEAD, cols)], 2)
    y0, high, low = call(
        first_kernel, [head, rhs, partner, f0, f3, high, low], [block, parts, parts], aliases={5: 1, 6: 2}
    )

    far = send(y0, 4)
    near = [send(y0, k) for k in (1, 2, 3)]
    ys = [y0] + near + [far] + [send(far, k) for k in (1, 2, 3)]
    facts, at_middle, at_spread, at_end = find_facts(near[0], parent, bounds, slot, structure, mask_table())
    t, y1 = call(second_kernel, [head, facts, rhs, high, low] + ys, [block, block])

    def middle(mask, head, high, low, t, y1):
        if not mask:
            return unread(block, 1)[0]
        if mask == n_row:
            return keep([y1])[0]
        return call(partner_kernel, [head, high, low, y1, send(t, mask)], [block])[0]

    fixed = lax.switch(
        at_middle[0], [functools.partial(middle, k) for k in range(n_row + 1)], head, high, low, t, y1
    )

    def spread(masks, y, fixed):
        blocks = keep([send(y if masks in MASK_PAIRS else fixed, k) for k in masks])
        return tuple([*blocks, *unread(block, 4 - len(masks))])

    zs = lax.switch(at_spread[0], [functools.partial(spread, masks) for masks in MASK_PAIRS + MASK_SETS], y1, fixed)
    def end(mask, head, facts, high, low, t, y0, y1, fixed, *zs):
        if mask == 0:
            return call(third_kernel, [head, facts, high, low, t, y0, y1, *zs[:2]], [block])[0]
        if mask is None:
            return call(third_kernel, [head, facts, high, low, t, y0, fixed, *zs], [block])[0]
        (total,) = call(residual_kernel, [facts, high, low, t, *zs], [block])
        return call(last_kernel, [head, high, low, y0, y1, total, send(total, mask)], [block])[0]

    return lax.switch(
        at_end[0],
        [functools.partial(end, k) for k in [0, None] + list(range(1, n_row))],
        *(head, facts, high, low, t, y0, y1, fixed, *zs),
    )


def body(factor, rhs, parent, bounds, slot, structure, n_row, n_col):
    count = slot.shape[0]
    if count == 8 and n_row == 8 and n_col == 4 and bounds.shape[0] == 8:
        return wide_body(factor, rhs, parent, bounds, slot, structure, n_row, n_col)
    return general_body(factor, rhs, parent, bounds, slot, structure, n_row)


def solution(mesh):
    in_specs = (P("row", "col"), P("row", "col"), P(), P(), P(), P())
    out_specs = P("row", "col")
    step = functools.partial(body, n_row=mesh.shape["row"], n_col=mesh.shape["col"])
    return jax.shard_map(step, mesh=mesh, in_specs=in_specs, out_specs=out_specs, check_vma=False)
```

```python
import functools
import itertools
import operator

import jax
import jax.numpy as jnp
import numpy as np
from jax import lax
from jax.experimental import pallas as pl
from jax.experimental.pallas import tpu as pltpu
from jax.sharding import PartitionSpec as P

SMEM = pl.BlockSpec(memory_space=pltpu.SMEM)
VMEM = pl.BlockSpec(memory_space=pltpu.VMEM)
ANY = pl.BlockSpec(memory_space=pl.ANY)
HIGHEST = lax.Precision.HIGHEST
F32 = jnp.float32
BF16 = jnp.bfloat16
SMALL = pltpu.CompilerParams(vmem_limit_bytes=4 * 1024 * 1024)


def block_masks(parent, bounds, slot, structure):
    count = slot.shape[0]
    ar = jnp.arange(count, dtype=jnp.int32)
    logical = jnp.sum(jnp.where(slot[:, None] == ar[None, :], ar[:, None], 0), axis=0)
    node = jnp.sum((logical[:, None] >= bounds[None, 1:7]).astype(jnp.int32), axis=1)
    level = (node >= 4).astype(jnp.int32) + (node >= 6).astype(jnp.int32)
    nodes = jnp.arange(7, dtype=jnp.int32)
    grand = parent[parent]
    ancestor = ((nodes[None, :] == parent[:, None]) | (nodes[None, :] == grand[:, None])) & (
        nodes[None, :] != nodes[:, None]
    )
    node_hot = (node[:, None] == nodes[None, :]).astype(jnp.float32)
    perm_hot = (logical[:, None] == ar[None, :]).astype(jnp.float32)
    listed_store = jnp.dot(structure.astype(jnp.float32), perm_hot.T, precision=HIGHEST)
    anc_pairs = jnp.dot(
        node_hot, jnp.dot(ancestor.astype(jnp.float32), node_hot.T, precision=HIGHEST), precision=HIGHEST
    )
    list_pairs = jnp.dot(node_hot, listed_store, precision=HIGHEST)
    link = (anc_pairs * list_pairs).T > 0.5
    same = node[:, None] == node[None, :]
    return level, same, link


def masked(block_rows, mask):
    rblocks, width = mask.shape
    bsz = block_rows.shape[0] // rblocks
    shaped = block_rows.reshape(rblocks, bsz, width, bsz) * mask[:, None, :, None].astype(jnp.float32)
    return shaped.reshape(block_rows.shape)


def general_body(factor, rhs, parent, bounds, slot, structure, n_row):
    level, same, link = block_masks(parent, bounds, slot, structure)
    held = slot.shape[0] // n_row
    bsz = factor.shape[0] // held
    first = lax.axis_index("row") * held
    level_mine = lax.dynamic_slice_in_dim(level, first, held, 0)
    same_mine = lax.dynamic_slice_in_dim(same, first, held, 0)
    link_mine = lax.dynamic_slice_in_dim(link, first, held, 0)
    full_rows = lax.all_gather(factor, "col", axis=1, tiled=True)
    diag_part = masked(full_rows, same_mine)
    link_part = masked(full_rows, link_mine)

    def product(matrix, vector):
        return jnp.dot(
            matrix,
            lax.all_gather(vector, "row", axis=0, tiled=True),
            precision=HIGHEST,
            preferred_element_type=jnp.float32,
        )

    acc = jnp.zeros(rhs.shape, jnp.float32)
    result = jnp.zeros(rhs.shape, jnp.float32)
    for section in range(3):
        rows = jnp.repeat(level_mine == section, bsz)[:, None]
        solved = jnp.where(rows, product(diag_part, rhs - acc), 0.0)
        result = result + solved
        if section < 2:
            acc = acc + product(link_part, solved)
    return result


ON = 0
SAME = 3
PARTNER = 8
HEAD = 16
LINK0 = 0
LINK1 = 8
FACTS = 40

MASK_PAIRS = list(itertools.combinations(range(1, 8), 2))
MASK_SETS = [
    s for size in (3, 4) for s in itertools.combinations(range(1, 8), size) if functools.reduce(operator.xor, s) == 0
]


def mask_table():
    table = np.zeros(256, np.int32)
    for i, masks in enumerate(MASK_PAIRS + MASK_SETS):
        table[sum(1 << k for k in masks)] = i
    return table


def as_int(flag):
    return jnp.where(flag, jnp.int32(1), jnp.int32(0))


def fetch(pairs, sems):
    copies = [pltpu.make_async_copy(a, b, sems.at[i]) for i, (a, b) in enumerate(pairs)]
    for copy in copies:
        copy.start()
    for copy in copies:
        copy.wait()


def wide_block(bounds):
    wide = jnp.int32(0)
    for s in range(1, 7):
        wide = wide + as_int(bounds[s] == s)
    return wide


def level_of(node):
    return as_int(node >= 4) + as_int(node >= 6)


def set_row(masks, row, flag):
    masks[row : row + 1, :] = jnp.full((1, masks.shape[1]), as_int(flag).astype(F32))


def split_piece(j, piece, high, low):
    bsz = piece.shape[0]
    for h in range(2):
        high[2 * j + h], low[2 * j + h] = split(piece[:, h * bsz : (h + 1) * bsz])


def head_kernel(both, first, masks):
    bounds, slot = both.at[:8], both.at[8:]
    p = lax.axis_index("row")
    wide = wide_block(bounds)
    m = slot[wide] ^ slot[wide + 1]
    first[...] = jnp.full(first.shape, jnp.where(wide < 4, m, 0))
    place = jnp.int32(0)
    for i in range(1, 8):
        place = place + i * as_int(slot[i] == p)
    node = place - as_int(place > wide)
    masks[...] = jnp.zeros(masks.shape, F32)
    for k in range(3):
        set_row(masks, ON + k, level_of(node) == k)
    set_row(masks, SAME, node == wide)
    for k in range(8):
        set_row(masks, PARTNER + k, (node == wide) & (place_of(m) == k))


def facts_kernel(after, parent_in, bounds_in, slot_in, structure_in, table_in, masks, middle, spread, end, parent, bounds, slot, structure, table, logical, node, link1, sems):
    del after
    pairs = [(parent_in, parent), (bounds_in, bounds), (slot_in, slot), (structure_in, structure), (table_in, table)]
    fetch(pairs, sems)
    p = lax.axis_index("row")
    c = lax.axis_index("col")
    wide = wide_block(bounds)
    wide_level = level_of(wide)
    m = slot[wide] ^ slot[wide + 1]
    for i in range(8):
        q = slot[i]
        logical[q] = i
        node[q] = i - as_int(i > wide)
    mine = node[p]
    place = logical[p]

    def linked(q):
        below = node[q]
        up = parent[below]
        top = parent[up]
        above = ((mine == up) | (mine == top)) & (mine != below)
        return above & (structure[below, place] == 1)

    masks[...] = jnp.zeros(masks.shape, F32)
    for k in range(8):
        q = k ^ (2 * c)
        on = linked(q)
        set_row(masks, LINK0 + k, on & (node[q] < 4))
        link1[k] = as_int(on & (node[q] >= 4) & (node[q] < 6))
    at_one = wide_level == 1
    at_two = wide_level == 2
    top = slot[7]
    u = slot[jnp.where(at_two, 4, 5)] ^ top
    v = slot[jnp.where(at_two, 5, 6)] ^ top
    third = slot[4] ^ top
    fourth = u ^ v ^ third
    one = jnp.int32(1)
    bits = (one << u) | (one << v)
    bits = bits | jnp.where(at_one, (one << third) | ((one << fourth) & 254), 0)
    bits = bits | jnp.where(at_two, (one << (u ^ m)) | (one << (v ^ m)), 0)

    def set_index(index, value):
        index[...] = jnp.full(index.shape, value)

    set_index(middle, jnp.where(at_one, m, jnp.where(at_two, 8, 0)))
    set_index(spread, table[bits])
    set_index(end, jnp.where(at_one, 1, jnp.where(at_two, 1 + m, 0)))

    def set_link(s, mask, on):
        at = place_of(mask)

        @pl.when(on)
        def _():
            row = LINK1 + 8 * s + at
            masks[pl.ds(row, 1), :] = jnp.full((1, masks.shape[1]), link1[at].astype(F32))

    count = jnp.int32(0)
    for k in range(1, 8):
        on = (bits >> k) & 1
        set_link(count, k, on == 1)
        count = count + on


def split(value):
    high = value.astype(BF16)
    return high, (value - high.astype(F32)).astype(BF16)


def dot(high, low, value):
    value_high, value_low = split(value)
    small = jnp.dot(high, value_low, preferred_element_type=F32) + jnp.dot(low, value_high, preferred_element_type=F32)
    return jnp.dot(high, value_high, preferred_element_type=F32) + small


def place_of(mask):
    return lax.axis_index("row") ^ mask ^ (2 * lax.axis_index("col"))


def row_of(masks, row):
    return masks[row : row + 1, :]


def own_part(head, high, low, level, mine):
    at = place_of(0)
    return dot(high[at], low[at], mine) * row_of(head, ON + level)


def partner_part(head, high, low, level, partner):
    on = row_of(head, SAME) * row_of(head, ON + level)
    block = [jnp.zeros(high.shape[1:], BF16) for _ in range(2)]
    for k in range(8):
        pick = row_of(head, PARTNER + k).astype(BF16)
        block = [block[0] + high[k] * pick, block[1] + low[k] * pick]
    return dot(block[0], block[1], jnp.where(on > 0, partner, 0.0))


def split_kernel(f1, f2, high, low):
    split_piece(1, f1, high, low)
    split_piece(2, f2, high, low)


def first_kernel(head, rhs, partner, f0, f3, high_in, low_in, y, high, low):
    del high_in, low_in
    split_piece(0, f0, high, low)
    split_piece(3, f3, high, low)
    y[...] = own_part(head, high, low, 0, rhs[...]) + partner_part(head, high, low, 0, partner[...])


def unread_kernel(*outs):
    del outs


def second_kernel(head, facts, rhs, high, low, *rest):
    ys, (t, y) = rest[:-2], rest[-2:]
    total = rhs[...]
    for k, block in enumerate(ys):
        at = place_of(k)
        total = total - dot(high[at], low[at], block[...] * facts[pl.ds(LINK0 + at, 1), :])
    t[...] = total
    y[...] = own_part(head, high, low, 1, total)


def partner_kernel(head, high, low, y_in, partner, y):
    y[...] = y_in[...] + partner_part(head, high, low, 1, partner[...])


def keep_kernel(*refs):
    half = len(refs) // 2
    for given, kept in zip(refs[:half], refs[half:]):
        kept[...] = given[...]


def less_linked(facts, high, low, t, zs):
    total = t
    for k in range(8):
        value = jnp.zeros(t.shape, F32)
        for s, z in enumerate(zs):
            value = value + jnp.where(row_of(facts, LINK1 + 8 * s + k) > 0, z, 0.0)
        total = total - dot(high[k], low[k], value)
    return total


def residual_kernel(facts, high, low, t, z0, z1, z2, z3, total):
    total[...] = less_linked(facts, high, low, t[...], [z0[...], z1[...], z2[...], z3[...]])


def last_kernel(head, high, low, y0, y1, total, partner, out):
    y2 = own_part(head, high, low, 2, total[...]) + partner_part(head, high, low, 2, partner[...])
    out[...] = y0[...] + y1[...] + y2


def third_kernel(head, facts, high, low, t, y0, y1, *rest):
    zs, out = rest[:-1], rest[-1]
    total = less_linked(facts, high, low, t[...], [z[...] for z in zs])
    out[...] = y0[...] + y1[...] + own_part(head, high, low, 2, total)


def call(kernel, args, outs, aliases=()):
    outs = [jax.ShapeDtypeStruct(*o) if isinstance(o[0], tuple) else jax.ShapeDtypeStruct(o, F32) for o in outs]
    return pl.pallas_call(
        kernel,
        in_specs=[VMEM] * len(args),
        out_specs=[VMEM] * len(outs),
        out_shape=outs,
        input_output_aliases=dict(aliases),
        compiler_params=SMALL,
    )(*args)


def keep(blocks):
    return call(keep_kernel, blocks, [b.shape for b in blocks])


def unread(shape, count):
    if not count:
        return ()
    outs = [jax.ShapeDtypeStruct(shape, F32)] * count
    return pl.pallas_call(unread_kernel, out_specs=[ANY] * count, out_shape=outs, compiler_params=SMALL)()


def find_facts(after, parent, bounds, slot, structure, table):
    i32 = jnp.int32
    args = [parent, bounds, slot, structure, jnp.asarray(table)]
    index = jax.ShapeDtypeStruct((128,), i32)
    return pl.pallas_call(
        facts_kernel,
        in_specs=[ANY] * 6,
        out_specs=[VMEM] * 4,
        out_shape=[jax.ShapeDtypeStruct((FACTS, 128), F32), index, index, index],
        scratch_shapes=[pltpu.SMEM(a.shape, i32) for a in args]
        + [pltpu.SMEM((8,), i32)] * 3
        + [pltpu.SemaphoreType.DMA((5,))],
        compiler_params=SMALL,
    )(after, *args)


def find_head(bounds, slot):
    outs = [jax.ShapeDtypeStruct((128,), jnp.int32), jax.ShapeDtypeStruct((HEAD, 128), F32)]
    both = jnp.concatenate([bounds, slot])
    return pl.pallas_call(
        head_kernel, in_specs=[SMEM], out_specs=[VMEM] * 2, out_shape=outs, compiler_params=SMALL
    )(both)


def wide_body(factor, rhs, parent, bounds, slot, structure, n_row, n_col):
    bsz, cols = rhs.shape
    block = (bsz, cols)

    def send(value, row_mask, col_mask=0):
        pairs = [
            (r * n_col + k, (r ^ row_mask) * n_col + (k ^ col_mask)) for r in range(n_row) for k in range(n_col)
        ]
        return lax.ppermute(value, ("row", "col"), pairs)

    first, head = find_head(bounds, slot)
    factor, rhs, first = lax.optimization_barrier((factor, rhs, first))
    f0 = factor
    f2 = send(f0, 0, 2)
    f1 = send(f0, 0, 1)

    def exchange(mask, value):
        return keep([send(value, mask)])[0] if mask else unread(block, 1)[0]

    partner = lax.switch(first[0], [functools.partial(exchange, k) for k in range(n_row)], rhs)
    f2, partner = lax.optimization_barrier((f2, partner))
    f3 = send(f2, 0, 1)
    parts = ((n_row, bsz, bsz), BF16)
    high, low = call(split_kernel, [f1, f2], [parts, parts])
    y0, high, low = call(
        first_kernel, [head, rhs, partner, f0, f3, high, low], [block, parts, parts], {5: 1, 6: 2}
    )

    far = send(y0, 4)
    near = [send(y0, k) for k in (1, 2, 3)]
    ys = [y0] + near + [far] + [send(far, k) for k in (1, 2, 3)]
    facts, at_middle, at_spread, at_end = find_facts(near[0], parent, bounds, slot, structure, mask_table())
    t, y1 = call(second_kernel, [head, facts, rhs, high, low] + ys, [block, block])

    def middle(mask, head, high, low, t, y1):
        if not mask:
            return unread(block, 1)[0]
        if mask == n_row:
            return keep([y1])[0]
        return call(partner_kernel, [head, high, low, y1, send(t, mask)], [block])[0]

    fixed = lax.switch(
        at_middle[0], [functools.partial(middle, k) for k in range(n_row + 1)], head, high, low, t, y1
    )

    def spread(masks, y, fixed):
        blocks = keep([send(y if masks in MASK_PAIRS else fixed, k) for k in masks])
        return tuple([*blocks, *unread(block, 4 - len(masks))])

    zs = lax.switch(at_spread[0], [functools.partial(spread, masks) for masks in MASK_PAIRS + MASK_SETS], y1, fixed)
    def end(mask, head, facts, high, low, t, y0, y1, fixed, *zs):
        if mask == 0:
            return call(third_kernel, [head, facts, high, low, t, y0, y1, *zs[:2]], [block])[0]
        if mask is None:
            return call(third_kernel, [head, facts, high, low, t, y0, fixed, *zs], [block])[0]
        (total,) = call(residual_kernel, [facts, high, low, t, *zs], [block])
        return call(last_kernel, [head, high, low, y0, y1, total, send(total, mask)], [block])[0]

    return lax.switch(
        at_end[0],
        [functools.partial(end, k) for k in [0, None] + list(range(1, n_row))],
        *(head, facts, high, low, t, y0, y1, fixed, *zs),
    )


def body(factor, rhs, parent, bounds, slot, structure, n_row, n_col):
    count = slot.shape[0]
    if count == 8 and n_row == 8 and n_col == 4 and bounds.shape[0] == 8:
        return wide_body(factor, rhs, parent, bounds, slot, structure, n_row, n_col)
    return general_body(factor, rhs, parent, bounds, slot, structure, n_row)


def solution(mesh):
    in_specs = (P("row", "col"), P("row", "col"), P(), P(), P(), P())
    out_specs = P("row", "col")
    step = functools.partial(body, n_row=mesh.shape["row"], n_col=mesh.shape["col"])
    return jax.shard_map(step, mesh=mesh, in_specs=in_specs, out_specs=out_specs, check_vma=False)
```

```python
import functools
import itertools
import operator

import jax
import jax.numpy as jnp
import numpy as np
from jax import lax
from jax.experimental import pallas as pl
from jax.experimental.pallas import tpu as pltpu
from jax.sharding import PartitionSpec as P

SMEM = pl.BlockSpec(memory_space=pltpu.SMEM)
VMEM = pl.BlockSpec(memory_space=pltpu.VMEM)
ANY = pl.BlockSpec(memory_space=pl.ANY)
HIGHEST = lax.Precision.HIGHEST
F32 = jnp.float32
BF16 = jnp.bfloat16
SMALL = pltpu.CompilerParams(vmem_limit_bytes=4 * 1024 * 1024)


def block_masks(parent, bounds, slot, structure):
    count = slot.shape[0]
    ar = jnp.arange(count, dtype=jnp.int32)
    logical = jnp.sum(jnp.where(slot[:, None] == ar[None, :], ar[:, None], 0), axis=0)
    node = jnp.sum((logical[:, None] >= bounds[None, 1:7]).astype(jnp.int32), axis=1)
    level = (node >= 4).astype(jnp.int32) + (node >= 6).astype(jnp.int32)
    nodes = jnp.arange(7, dtype=jnp.int32)
    grand = parent[parent]
    ancestor = ((nodes[None, :] == parent[:, None]) | (nodes[None, :] == grand[:, None])) & (
        nodes[None, :] != nodes[:, None]
    )
    node_hot = (node[:, None] == nodes[None, :]).astype(jnp.float32)
    perm_hot = (logical[:, None] == ar[None, :]).astype(jnp.float32)
    listed_store = jnp.dot(structure.astype(jnp.float32), perm_hot.T, precision=HIGHEST)
    anc_pairs = jnp.dot(
        node_hot, jnp.dot(ancestor.astype(jnp.float32), node_hot.T, precision=HIGHEST), precision=HIGHEST
    )
    list_pairs = jnp.dot(node_hot, listed_store, precision=HIGHEST)
    link = (anc_pairs * list_pairs).T > 0.5
    same = node[:, None] == node[None, :]
    return level, same, link


def masked(block_rows, mask):
    rblocks, width = mask.shape
    bsz = block_rows.shape[0] // rblocks
    shaped = block_rows.reshape(rblocks, bsz, width, bsz) * mask[:, None, :, None].astype(jnp.float32)
    return shaped.reshape(block_rows.shape)


def general_body(factor, rhs, parent, bounds, slot, structure, n_row):
    level, same, link = block_masks(parent, bounds, slot, structure)
    held = slot.shape[0] // n_row
    bsz = factor.shape[0] // held
    first = lax.axis_index("row") * held
    level_mine = lax.dynamic_slice_in_dim(level, first, held, 0)
    same_mine = lax.dynamic_slice_in_dim(same, first, held, 0)
    link_mine = lax.dynamic_slice_in_dim(link, first, held, 0)
    full_rows = lax.all_gather(factor, "col", axis=1, tiled=True)
    diag_part = masked(full_rows, same_mine)
    link_part = masked(full_rows, link_mine)

    def product(matrix, vector):
        return jnp.dot(
            matrix,
            lax.all_gather(vector, "row", axis=0, tiled=True),
            precision=HIGHEST,
            preferred_element_type=jnp.float32,
        )

    acc = jnp.zeros(rhs.shape, jnp.float32)
    result = jnp.zeros(rhs.shape, jnp.float32)
    for section in range(3):
        rows = jnp.repeat(level_mine == section, bsz)[:, None]
        solved = jnp.where(rows, product(diag_part, rhs - acc), 0.0)
        result = result + solved
        if section < 2:
            acc = acc + product(link_part, solved)
    return result


ON = 0
SAME = 3
PARTNER = 8
HEAD = 16
LINK0 = 0
LINK1 = 8
FACTS = 40

MASK_PAIRS = list(itertools.combinations(range(1, 8), 2))
MASK_SETS = [
    s for size in (3, 4) for s in itertools.combinations(range(1, 8), size) if functools.reduce(operator.xor, s) == 0
]


def mask_table():
    table = np.zeros(256, np.int32)
    for i, masks in enumerate(MASK_PAIRS + MASK_SETS):
        table[sum(1 << k for k in masks)] = i
    return table


def as_int(flag):
    return jnp.where(flag, jnp.int32(1), jnp.int32(0))


def fetch(pairs, sems):
    copies = [pltpu.make_async_copy(a, b, sems.at[i]) for i, (a, b) in enumerate(pairs)]
    for copy in copies:
        copy.start()
    for copy in copies:
        copy.wait()


def wide_block(bounds):
    wide = jnp.int32(0)
    for s in range(1, 7):
        wide = wide + as_int(bounds[s] == s)
    return wide


def level_of(node):
    return as_int(node >= 4) + as_int(node >= 6)


def set_row(masks, row, flag):
    masks[row : row + 1, :] = jnp.full((1, masks.shape[1]), as_int(flag).astype(F32))


def split_piece(j, piece, high, low):
    bsz = piece.shape[0]
    for h in range(2):
        high[2 * j + h], low[2 * j + h] = split(piece[:, h * bsz : (h + 1) * bsz])


def head_kernel(both, first, masks):
    bounds, slot = both.at[:8], both.at[8:]
    p = lax.axis_index("row")
    wide = wide_block(bounds)
    m = slot[wide] ^ slot[wide + 1]
    first[...] = jnp.full(first.shape, jnp.where(wide < 4, m, 0))
    place = jnp.int32(0)
    for i in range(1, 8):
        place = place + i * as_int(slot[i] == p)
    node = place - as_int(place > wide)
    masks[...] = jnp.zeros(masks.shape, F32)
    for k in range(3):
        set_row(masks, ON + k, level_of(node) == k)
    set_row(masks, SAME, node == wide)
    for k in range(8):
        set_row(masks, PARTNER + k, (node == wide) & (place_of(m) == k))


def facts_kernel(after, parent_in, bounds_in, slot_in, structure_in, table_in, masks, middle, spread, end, parent, bounds, slot, structure, table, logical, node, link1, sems):
    del after
    pairs = [(parent_in, parent), (bounds_in, bounds), (slot_in, slot), (structure_in, structure), (table_in, table)]
    fetch(pairs, sems)
    p = lax.axis_index("row")
    c = lax.axis_index("col")
    wide = wide_block(bounds)
    wide_level = level_of(wide)
    m = slot[wide] ^ slot[wide + 1]
    for i in range(8):
        q = slot[i]
        logical[q] = i
        node[q] = i - as_int(i > wide)
    mine = node[p]
    place = logical[p]

    def linked(q):
        below = node[q]
        up = parent[below]
        top = parent[up]
        above = ((mine == up) | (mine == top)) & (mine != below)
        return above & (structure[below, place] == 1)

    masks[...] = jnp.zeros(masks.shape, F32)
    for k in range(8):
        q = k ^ (2 * c)
        on = linked(q)
        set_row(masks, LINK0 + k, on & (node[q] < 4))
        link1[k] = as_int(on & (node[q] >= 4) & (node[q] < 6))
    at_one = wide_level == 1
    at_two = wide_level == 2
    top = slot[7]
    u = slot[jnp.where(at_two, 4, 5)] ^ top
    v = slot[jnp.where(at_two, 5, 6)] ^ top
    third = slot[4] ^ top
    fourth = u ^ v ^ third
    one = jnp.int32(1)
    bits = (one << u) | (one << v)
    bits = bits | jnp.where(at_one, (one << third) | ((one << fourth) & 254), 0)
    bits = bits | jnp.where(at_two, (one << (u ^ m)) | (one << (v ^ m)), 0)

    def set_index(index, value):
        index[...] = jnp.full(index.shape, value)

    set_index(middle, jnp.where(at_one, m, jnp.where(at_two, 8, 0)))
    set_index(spread, table[bits])
    set_index(end, jnp.where(at_one, 1, jnp.where(at_two, 1 + m, 0)))

    def set_link(s, mask, on):
        at = place_of(mask)

        @pl.when(on)
        def _():
            row = LINK1 + 8 * s + at
            masks[pl.ds(row, 1), :] = jnp.full((1, masks.shape[1]), link1[at].astype(F32))

    count = jnp.int32(0)
    for k in range(1, 8):
        on = (bits >> k) & 1
        set_link(count, k, on == 1)
        count = count + on


def split(value):
    high = value.astype(BF16)
    return high, (value - high.astype(F32)).astype(BF16)


def dot(high, low, value):
    value_high, value_low = split(value)
    small = jnp.dot(high, value_low, preferred_element_type=F32) + jnp.dot(low, value_high, preferred_element_type=F32)
    return jnp.dot(high, value_high, preferred_element_type=F32) + small


def place_of(mask):
    return lax.axis_index("row") ^ mask ^ (2 * lax.axis_index("col"))


def row_of(masks, row):
    return masks[row : row + 1, :]


def own_part(head, high, low, level, mine):
    at = place_of(0)
    return dot(high[at], low[at], mine) * row_of(head, ON + level)


def partner_part(head, high, low, level, partner):
    on = row_of(head, SAME) * row_of(head, ON + level)
    block = [jnp.zeros(high.shape[1:], BF16) for _ in range(2)]
    for k in range(8):
        pick = row_of(head, PARTNER + k).astype(BF16)
        block = [block[0] + high[k] * pick, block[1] + low[k] * pick]
    return dot(block[0], block[1], jnp.where(on > 0, partner, 0.0))


def split_kernel(f1, f2, high, low):
    split_piece(1, f1, high, low)
    split_piece(2, f2, high, low)


def first_kernel(head, rhs, partner, f0, f3, high_in, low_in, y, high, low):
    del high_in, low_in
    split_piece(0, f0, high, low)
    split_piece(3, f3, high, low)
    y[...] = own_part(head, high, low, 0, rhs[...]) + partner_part(head, high, low, 0, partner[...])


def unread_kernel(*outs):
    del outs


def second_kernel(head, facts, rhs, high, low, *rest):
    ys, (t, y) = rest[:-2], rest[-2:]
    total = rhs[...]
    for k, block in enumerate(ys):
        at = place_of(k)
        total = total - dot(high[at], low[at], block[...] * facts[pl.ds(LINK0 + at, 1), :])
    t[...] = total
    y[...] = own_part(head, high, low, 1, total)


def partner_kernel(head, high, low, y_in, partner, y):
    y[...] = y_in[...] + partner_part(head, high, low, 1, partner[...])


def keep_kernel(*refs):
    half = len(refs) // 2
    for given, kept in zip(refs[:half], refs[half:]):
        kept[...] = given[...]


def less_linked(facts, high, low, t, zs):
    total = t
    for k in range(8):
        value = jnp.zeros(t.shape, F32)
        for s, z in enumerate(zs):
            value = value + jnp.where(row_of(facts, LINK1 + 8 * s + k) > 0, z, 0.0)
        total = total - dot(high[k], low[k], value)
    return total


def residual_kernel(facts, high, low, t, z0, z1, z2, z3, total):
    total[...] = less_linked(facts, high, low, t[...], [z0[...], z1[...], z2[...], z3[...]])


def last_kernel(head, high, low, y0, y1, total, partner, out):
    y2 = own_part(head, high, low, 2, total[...]) + partner_part(head, high, low, 2, partner[...])
    out[...] = y0[...] + y1[...] + y2


def third_kernel(head, facts, high, low, t, y0, y1, *rest):
    zs, out = rest[:-1], rest[-1]
    total = less_linked(facts, high, low, t[...], [z[...] for z in zs])
    out[...] = y0[...] + y1[...] + own_part(head, high, low, 2, total)


def call(kernel, args, outs, aliases=()):
    outs = [jax.ShapeDtypeStruct(*o) if isinstance(o[0], tuple) else jax.ShapeDtypeStruct(o, F32) for o in outs]
    return pl.pallas_call(
        kernel,
        in_specs=[VMEM] * len(args),
        out_specs=[VMEM] * len(outs),
        out_shape=outs,
        input_output_aliases=dict(aliases),
        compiler_params=SMALL,
    )(*args)


def keep(blocks):
    return call(keep_kernel, blocks, [b.shape for b in blocks])


def unread(shape, count):
    if not count:
        return ()
    outs = [jax.ShapeDtypeStruct(shape, F32)] * count
    return pl.pallas_call(unread_kernel, out_specs=[ANY] * count, out_shape=outs, compiler_params=SMALL)()


def find_facts(after, parent, bounds, slot, structure, table):
    i32 = jnp.int32
    args = [parent, bounds, slot, structure, jnp.asarray(table)]
    index = jax.ShapeDtypeStruct((128,), i32)
    return pl.pallas_call(
        facts_kernel,
        in_specs=[ANY] * 6,
        out_specs=[VMEM] * 4,
        out_shape=[jax.ShapeDtypeStruct((FACTS, 128), F32), index, index, index],
        scratch_shapes=[pltpu.SMEM(a.shape, i32) for a in args]
        + [pltpu.SMEM((8,), i32)] * 3
        + [pltpu.SemaphoreType.DMA((5,))],
        compiler_params=SMALL,
    )(after, *args)


def find_head(bounds, slot):
    outs = [jax.ShapeDtypeStruct((128,), jnp.int32), jax.ShapeDtypeStruct((HEAD, 128), F32)]
    both = jnp.concatenate([bounds, slot])
    return pl.pallas_call(
        head_kernel, in_specs=[SMEM], out_specs=[VMEM] * 2, out_shape=outs, compiler_params=SMALL
    )(both)


def wide_body(factor, rhs, parent, bounds, slot, structure, n_row, n_col):
    bsz, cols = rhs.shape
    block = (bsz, cols)

    def send(value, row_mask, col_mask=0):
        pairs = [
            (r * n_col + k, (r ^ row_mask) * n_col + (k ^ col_mask)) for r in range(n_row) for k in range(n_col)
        ]
        return lax.ppermute(value, ("row", "col"), pairs)

    f0 = factor
    f2 = send(f0, 0, 2)
    first, head = find_head(bounds, slot)
    f1 = send(f0, 0, 1)

    def exchange(mask, value):
        return keep([send(value, mask)])[0] if mask else unread(block, 1)[0]

    partner = lax.switch(first[0], [functools.partial(exchange, k) for k in range(n_row)], rhs)
    f2, partner = lax.optimization_barrier((f2, partner))
    f3 = send(f2, 0, 1)
    parts = ((n_row, bsz, bsz), BF16)
    high, low = call(split_kernel, [f1, f2], [parts, parts])
    y0, high, low = call(
        first_kernel, [head, rhs, partner, f0, f3, high, low], [block, parts, parts], {5: 1, 6: 2}
    )

    far = send(y0, 4)
    near = [send(y0, k) for k in (1, 2, 3)]
    ys = [y0] + near + [far] + [send(far, k) for k in (1, 2, 3)]
    facts, at_middle, at_spread, at_end = find_facts(near[0], parent, bounds, slot, structure, mask_table())
    t, y1 = call(second_kernel, [head, facts, rhs, high, low] + ys, [block, block])

    def middle(mask, head, high, low, t, y1):
        if not mask:
            return unread(block, 1)[0]
        if mask == n_row:
            return keep([y1])[0]
        return call(partner_kernel, [head, high, low, y1, send(t, mask)], [block])[0]

    fixed = lax.switch(
        at_middle[0], [functools.partial(middle, k) for k in range(n_row + 1)], head, high, low, t, y1
    )

    def spread(masks, y, fixed):
        blocks = keep([send(y if masks in MASK_PAIRS else fixed, k) for k in masks])
        return tuple([*blocks, *unread(block, 4 - len(masks))])

    zs = lax.switch(at_spread[0], [functools.partial(spread, masks) for masks in MASK_PAIRS + MASK_SETS], y1, fixed)
    def end(mask, head, facts, high, low, t, y0, y1, fixed, *zs):
        if mask == 0:
            return call(third_kernel, [head, facts, high, low, t, y0, y1, *zs[:2]], [block])[0]
        if mask is None:
            return call(third_kernel, [head, facts, high, low, t, y0, fixed, *zs], [block])[0]
        (total,) = call(residual_kernel, [facts, high, low, t, *zs], [block])
        return call(last_kernel, [head, high, low, y0, y1, total, send(total, mask)], [block])[0]

    return lax.switch(
        at_end[0],
        [functools.partial(end, k) for k in [0, None] + list(range(1, n_row))],
        *(head, facts, high, low, t, y0, y1, fixed, *zs),
    )


def body(factor, rhs, parent, bounds, slot, structure, n_row, n_col):
    count = slot.shape[0]
    if count == 8 and n_row == 8 and n_col == 4 and bounds.shape[0] == 8:
        return wide_body(factor, rhs, parent, bounds, slot, structure, n_row, n_col)
    return general_body(factor, rhs, parent, bounds, slot, structure, n_row)


def solution(mesh):
    in_specs = (P("row", "col"), P("row", "col"), P(), P(), P(), P())
    out_specs = P("row", "col")
    step = functools.partial(body, n_row=mesh.shape["row"], n_col=mesh.shape["col"])
    return jax.shard_map(step, mesh=mesh, in_specs=in_specs, out_specs=out_specs, check_vma=False)
```

```python
import functools
import itertools
import operator

import jax
import jax.numpy as jnp
import numpy as np
from jax import lax
from jax.experimental import pallas as pl
from jax.experimental.pallas import tpu as pltpu
from jax.sharding import PartitionSpec as P

SMEM = pl.BlockSpec(memory_space=pltpu.SMEM)
VMEM = pl.BlockSpec(memory_space=pltpu.VMEM)
ANY = pl.BlockSpec(memory_space=pl.ANY)
HIGHEST = lax.Precision.HIGHEST
F32 = jnp.float32
BF16 = jnp.bfloat16
SMALL = pltpu.CompilerParams(vmem_limit_bytes=4 * 1024 * 1024)


def block_masks(parent, bounds, slot, structure):
    count = slot.shape[0]
    ar = jnp.arange(count, dtype=jnp.int32)
    logical = jnp.sum(jnp.where(slot[:, None] == ar[None, :], ar[:, None], 0), axis=0)
    node = jnp.sum((logical[:, None] >= bounds[None, 1:7]).astype(jnp.int32), axis=1)
    level = (node >= 4).astype(jnp.int32) + (node >= 6).astype(jnp.int32)
    nodes = jnp.arange(7, dtype=jnp.int32)
    grand = parent[parent]
    ancestor = ((nodes[None, :] == parent[:, None]) | (nodes[None, :] == grand[:, None])) & (
        nodes[None, :] != nodes[:, None]
    )
    node_hot = (node[:, None] == nodes[None, :]).astype(jnp.float32)
    perm_hot = (logical[:, None] == ar[None, :]).astype(jnp.float32)
    listed_store = jnp.dot(structure.astype(jnp.float32), perm_hot.T, precision=HIGHEST)
    anc_pairs = jnp.dot(
        node_hot, jnp.dot(ancestor.astype(jnp.float32), node_hot.T, precision=HIGHEST), precision=HIGHEST
    )
    list_pairs = jnp.dot(node_hot, listed_store, precision=HIGHEST)
    link = (anc_pairs * list_pairs).T > 0.5
    same = node[:, None] == node[None, :]
    return level, same, link


def masked(block_rows, mask):
    rblocks, width = mask.shape
    bsz = block_rows.shape[0] // rblocks
    shaped = block_rows.reshape(rblocks, bsz, width, bsz) * mask[:, None, :, None].astype(jnp.float32)
    return shaped.reshape(block_rows.shape)


def general_body(factor, rhs, parent, bounds, slot, structure, n_row):
    level, same, link = block_masks(parent, bounds, slot, structure)
    held = slot.shape[0] // n_row
    bsz = factor.shape[0] // held
    first = lax.axis_index("row") * held
    level_mine = lax.dynamic_slice_in_dim(level, first, held, 0)
    same_mine = lax.dynamic_slice_in_dim(same, first, held, 0)
    link_mine = lax.dynamic_slice_in_dim(link, first, held, 0)
    full_rows = lax.all_gather(factor, "col", axis=1, tiled=True)
    diag_part = masked(full_rows, same_mine)
    link_part = masked(full_rows, link_mine)

    def product(matrix, vector):
        return jnp.dot(
            matrix,
            lax.all_gather(vector, "row", axis=0, tiled=True),
            precision=HIGHEST,
            preferred_element_type=jnp.float32,
        )

    acc = jnp.zeros(rhs.shape, jnp.float32)
    result = jnp.zeros(rhs.shape, jnp.float32)
    for section in range(3):
        rows = jnp.repeat(level_mine == section, bsz)[:, None]
        solved = jnp.where(rows, product(diag_part, rhs - acc), 0.0)
        result = result + solved
        if section < 2:
            acc = acc + product(link_part, solved)
    return result


ON = 0
SAME = 3
PARTNER = 8
HEAD = 16
LINK0 = 0
LINK1 = 8
FACTS = 40

MASK_PAIRS = list(itertools.combinations(range(1, 8), 2))
MASK_SETS = [
    s for size in (3, 4) for s in itertools.combinations(range(1, 8), size) if functools.reduce(operator.xor, s) == 0
]


def mask_table():
    table = np.zeros(256, np.int32)
    for i, masks in enumerate(MASK_PAIRS + MASK_SETS):
        table[sum(1 << k for k in masks)] = i
    return table


def as_int(flag):
    return jnp.where(flag, jnp.int32(1), jnp.int32(0))


def fetch(pairs, sems):
    copies = [pltpu.make_async_copy(a, b, sems.at[i]) for i, (a, b) in enumerate(pairs)]
    for copy in copies:
        copy.start()
    for copy in copies:
        copy.wait()


def wide_block(bounds):
    wide = jnp.int32(0)
    for s in range(1, 7):
        wide = wide + as_int(bounds[s] == s)
    return wide


def level_of(node):
    return as_int(node >= 4) + as_int(node >= 6)


def set_row(masks, row, flag):
    masks[row : row + 1, :] = jnp.full((1, masks.shape[1]), as_int(flag).astype(F32))


def split_piece(j, piece, high, low):
    bsz = piece.shape[0]
    for h in range(2):
        high[2 * j + h], low[2 * j + h] = split(piece[:, h * bsz : (h + 1) * bsz])


def head_kernel(both, first, masks):
    bounds, slot = both.at[:8], both.at[8:]
    p = lax.axis_index("row")
    wide = wide_block(bounds)
    m = slot[wide] ^ slot[wide + 1]
    first[...] = jnp.full(first.shape, jnp.where(wide < 4, m, 0))
    place = jnp.int32(0)
    for i in range(1, 8):
        place = place + i * as_int(slot[i] == p)
    node = place - as_int(place > wide)
    masks[...] = jnp.zeros(masks.shape, F32)
    for k in range(3):
        set_row(masks, ON + k, level_of(node) == k)
    set_row(masks, SAME, node == wide)
    for k in range(8):
        set_row(masks, PARTNER + k, (node == wide) & (place_of(m) == k))


def facts_kernel(after, parent_in, bounds_in, slot_in, structure_in, table_in, masks, middle, spread, end, parent, bounds, slot, structure, table, logical, node, link1, sems):
    del after
    pairs = [(parent_in, parent), (bounds_in, bounds), (slot_in, slot), (structure_in, structure), (table_in, table)]
    fetch(pairs, sems)
    p = lax.axis_index("row")
    c = lax.axis_index("col")
    wide = wide_block(bounds)
    wide_level = level_of(wide)
    m = slot[wide] ^ slot[wide + 1]
    for i in range(8):
        q = slot[i]
        logical[q] = i
        node[q] = i - as_int(i > wide)
    mine = node[p]
    place = logical[p]

    def linked(q):
        below = node[q]
        up = parent[below]
        top = parent[up]
        above = ((mine == up) | (mine == top)) & (mine != below)
        return above & (structure[below, place] == 1)

    masks[...] = jnp.zeros(masks.shape, F32)
    for k in range(8):
        q = k ^ (2 * c)
        on = linked(q)
        set_row(masks, LINK0 + k, on & (node[q] < 4))
        link1[k] = as_int(on & (node[q] >= 4) & (node[q] < 6))
    at_one = wide_level == 1
    at_two = wide_level == 2
    top = slot[7]
    u = slot[jnp.where(at_two, 4, 5)] ^ top
    v = slot[jnp.where(at_two, 5, 6)] ^ top
    third = slot[4] ^ top
    fourth = u ^ v ^ third
    one = jnp.int32(1)
    bits = (one << u) | (one << v)
    bits = bits | jnp.where(at_one, (one << third) | ((one << fourth) & 254), 0)
    bits = bits | jnp.where(at_two, (one << (u ^ m)) | (one << (v ^ m)), 0)

    def set_index(index, value):
        index[...] = jnp.full(index.shape, value)

    set_index(middle, jnp.where(at_one, m, jnp.where(at_two, 8, 0)))
    set_index(spread, table[bits])
    set_index(end, jnp.where(at_one, 1, jnp.where(at_two, 1 + m, 0)))

    def set_link(s, mask, on):
        at = place_of(mask)

        @pl.when(on)
        def _():
            row = LINK1 + 8 * s + at
            masks[pl.ds(row, 1), :] = jnp.full((1, masks.shape[1]), link1[at].astype(F32))

    count = jnp.int32(0)
    for k in range(1, 8):
        on = (bits >> k) & 1
        set_link(count, k, on == 1)
        count = count + on


def split(value):
    high = value.astype(BF16)
    return high, (value - high.astype(F32)).astype(BF16)


def dot(high, low, value):
    value_high, value_low = split(value)
    small = jnp.dot(high, value_low, preferred_element_type=F32) + jnp.dot(low, value_high, preferred_element_type=F32)
    return jnp.dot(high, value_high, preferred_element_type=F32) + small


def dot_pair(high, low, places, blocks):
    both = [jnp.concatenate([part[places[0]], part[places[1]]], axis=1) for part in (high, low)]
    return dot(both[0], both[1], jnp.concatenate(blocks, axis=0))


def place_of(mask):
    return lax.axis_index("row") ^ mask ^ (2 * lax.axis_index("col"))


def row_of(masks, row):
    return masks[row : row + 1, :]


def own_part(head, high, low, level, mine):
    at = place_of(0)
    return dot(high[at], low[at], mine) * row_of(head, ON + level)


def partner_part(head, high, low, level, partner):
    on = row_of(head, SAME) * row_of(head, ON + level)
    block = [jnp.zeros(high.shape[1:], BF16) for _ in range(2)]
    for k in range(8):
        pick = row_of(head, PARTNER + k).astype(BF16)
        block = [block[0] + high[k] * pick, block[1] + low[k] * pick]
    return dot(block[0], block[1], jnp.where(on > 0, partner, 0.0))


def split_kernel(f1, f2, high, low):
    split_piece(1, f1, high, low)
    split_piece(2, f2, high, low)


def first_kernel(head, rhs, partner, f0, f3, high_in, low_in, y, high, low):
    del high_in, low_in
    split_piece(0, f0, high, low)
    split_piece(3, f3, high, low)
    y[...] = own_part(head, high, low, 0, rhs[...]) + partner_part(head, high, low, 0, partner[...])


def unread_kernel(*outs):
    del outs


def second_kernel(head, facts, rhs, high, low, *rest):
    ys, (t, y) = rest[:-2], rest[-2:]
    total = rhs[...]
    for k in range(0, 8, 2):
        places = [place_of(k), place_of(k + 1)]
        blocks = [ys[k + i][...] * facts[pl.ds(LINK0 + places[i], 1), :] for i in range(2)]
        total = total - dot_pair(high, low, places, blocks)
    t[...] = total
    y[...] = own_part(head, high, low, 1, total)


def partner_kernel(head, high, low, y_in, partner, y):
    y[...] = y_in[...] + partner_part(head, high, low, 1, partner[...])


def keep_kernel(*refs):
    half = len(refs) // 2
    for given, kept in zip(refs[:half], refs[half:]):
        kept[...] = given[...]


def less_linked(facts, high, low, t, zs):
    total = t
    for k in range(0, 8, 2):
        blocks = []
        for i in range(2):
            value = jnp.zeros(t.shape, F32)
            for s, z in enumerate(zs):
                value = value + jnp.where(row_of(facts, LINK1 + 8 * s + k + i) > 0, z, 0.0)
            blocks.append(value)
        total = total - dot_pair(high, low, [k, k + 1], blocks)
    return total


def residual_kernel(facts, high, low, t, z0, z1, z2, z3, total):
    total[...] = less_linked(facts, high, low, t[...], [z0[...], z1[...], z2[...], z3[...]])


def last_kernel(head, high, low, y0, y1, total, partner, out):
    y2 = own_part(head, high, low, 2, total[...]) + partner_part(head, high, low, 2, partner[...])
    out[...] = y0[...] + y1[...] + y2


def third_kernel(head, facts, high, low, t, y0, y1, *rest):
    zs, out = rest[:-1], rest[-1]
    total = less_linked(facts, high, low, t[...], [z[...] for z in zs])
    out[...] = y0[...] + y1[...] + own_part(head, high, low, 2, total)


def call(kernel, args, outs, aliases=()):
    outs = [jax.ShapeDtypeStruct(*o) if isinstance(o[0], tuple) else jax.ShapeDtypeStruct(o, F32) for o in outs]
    return pl.pallas_call(
        kernel,
        in_specs=[VMEM] * len(args),
        out_specs=[VMEM] * len(outs),
        out_shape=outs,
        input_output_aliases=dict(aliases),
        compiler_params=SMALL,
    )(*args)


def keep(blocks):
    return call(keep_kernel, blocks, [b.shape for b in blocks])


def unread(shape, count):
    if not count:
        return ()
    outs = [jax.ShapeDtypeStruct(shape, F32)] * count
    return pl.pallas_call(unread_kernel, out_specs=[ANY] * count, out_shape=outs, compiler_params=SMALL)()


def find_facts(after, parent, bounds, slot, structure, table):
    i32 = jnp.int32
    args = [parent, bounds, slot, structure, jnp.asarray(table)]
    index = jax.ShapeDtypeStruct((128,), i32)
    return pl.pallas_call(
        facts_kernel,
        in_specs=[ANY] * 6,
        out_specs=[VMEM] * 4,
        out_shape=[jax.ShapeDtypeStruct((FACTS, 128), F32), index, index, index],
        scratch_shapes=[pltpu.SMEM(a.shape, i32) for a in args]
        + [pltpu.SMEM((8,), i32)] * 3
        + [pltpu.SemaphoreType.DMA((5,))],
        compiler_params=SMALL,
    )(after, *args)


def find_head(bounds, slot):
    outs = [jax.ShapeDtypeStruct((128,), jnp.int32), jax.ShapeDtypeStruct((HEAD, 128), F32)]
    both = jnp.concatenate([bounds, slot])
    return pl.pallas_call(
        head_kernel, in_specs=[SMEM], out_specs=[VMEM] * 2, out_shape=outs, compiler_params=SMALL
    )(both)


def wide_body(factor, rhs, parent, bounds, slot, structure, n_row, n_col):
    bsz, cols = rhs.shape
    block = (bsz, cols)

    def send(value, row_mask, col_mask=0):
        pairs = [
            (r * n_col + k, (r ^ row_mask) * n_col + (k ^ col_mask)) for r in range(n_row) for k in range(n_col)
        ]
        return lax.ppermute(value, ("row", "col"), pairs)

    f0 = factor
    f2 = send(f0, 0, 2)
    first, head = find_head(bounds, slot)
    f1 = send(f0, 0, 1)

    def exchange(mask, value):
        return keep([send(value, mask)])[0] if mask else unread(block, 1)[0]

    partner = lax.switch(first[0], [functools.partial(exchange, k) for k in range(n_row)], rhs)
    f2, partner = lax.optimization_barrier((f2, partner))
    f3 = send(f2, 0, 1)
    parts = ((n_row, bsz, bsz), BF16)
    high, low = call(split_kernel, [f1, f2], [parts, parts])
    y0, high, low = call(
        first_kernel, [head, rhs, partner, f0, f3, high, low], [block, parts, parts], {5: 1, 6: 2}
    )

    far = send(y0, 4)
    near = [send(y0, k) for k in (1, 2, 3)]
    ys = [y0] + near + [far] + [send(far, k) for k in (1, 2, 3)]
    facts, at_middle, at_spread, at_end = find_facts(near[0], parent, bounds, slot, structure, mask_table())
    t, y1 = call(second_kernel, [head, facts, rhs, high, low] + ys, [block, block])

    def middle(mask, head, high, low, t, y1):
        if not mask:
            return unread(block, 1)[0]
        if mask == n_row:
            return keep([y1])[0]
        return call(partner_kernel, [head, high, low, y1, send(t, mask)], [block])[0]

    fixed = lax.switch(
        at_middle[0], [functools.partial(middle, k) for k in range(n_row + 1)], head, high, low, t, y1
    )

    def spread(masks, y, fixed):
        blocks = keep([send(y if masks in MASK_PAIRS else fixed, k) for k in masks])
        return tuple([*blocks, *unread(block, 4 - len(masks))])

    zs = lax.switch(at_spread[0], [functools.partial(spread, masks) for masks in MASK_PAIRS + MASK_SETS], y1, fixed)
    def end(mask, head, facts, high, low, t, y0, y1, fixed, *zs):
        if mask == 0:
            return call(third_kernel, [head, facts, high, low, t, y0, y1, *zs[:2]], [block])[0]
        if mask is None:
            return call(third_kernel, [head, facts, high, low, t, y0, fixed, *zs], [block])[0]
        (total,) = call(residual_kernel, [facts, high, low, t, *zs], [block])
        return call(last_kernel, [head, high, low, y0, y1, total, send(total, mask)], [block])[0]

    return lax.switch(
        at_end[0],
        [functools.partial(end, k) for k in [0, None] + list(range(1, n_row))],
        *(head, facts, high, low, t, y0, y1, fixed, *zs),
    )


def body(factor, rhs, parent, bounds, slot, structure, n_row, n_col):
    count = slot.shape[0]
    if count == 8 and n_row == 8 and n_col == 4 and bounds.shape[0] == 8:
        return wide_body(factor, rhs, parent, bounds, slot, structure, n_row, n_col)
    return general_body(factor, rhs, parent, bounds, slot, structure, n_row)


def solution(mesh):
    in_specs = (P("row", "col"), P("row", "col"), P(), P(), P(), P())
    out_specs = P("row", "col")
    step = functools.partial(body, n_row=mesh.shape["row"], n_col=mesh.shape["col"])
    return jax.shard_map(step, mesh=mesh, in_specs=in_specs, out_specs=out_specs, check_vma=False)
```

```python
import functools
import itertools
import operator

import jax
import jax.numpy as jnp
import numpy as np
from jax import lax
from jax.experimental import pallas as pl
from jax.experimental.pallas import tpu as pltpu
from jax.sharding import PartitionSpec as P

SMEM = pl.BlockSpec(memory_space=pltpu.SMEM)
VMEM = pl.BlockSpec(memory_space=pltpu.VMEM)
ANY = pl.BlockSpec(memory_space=pl.ANY)
HIGHEST = lax.Precision.HIGHEST
F32 = jnp.float32
BF16 = jnp.bfloat16
SMALL = pltpu.CompilerParams(vmem_limit_bytes=4 * 1024 * 1024)


def block_masks(parent, bounds, slot, structure):
    count = slot.shape[0]
    ar = jnp.arange(count, dtype=jnp.int32)
    logical = jnp.sum(jnp.where(slot[:, None] == ar[None, :], ar[:, None], 0), axis=0)
    node = jnp.sum((logical[:, None] >= bounds[None, 1:7]).astype(jnp.int32), axis=1)
    level = (node >= 4).astype(jnp.int32) + (node >= 6).astype(jnp.int32)
    nodes = jnp.arange(7, dtype=jnp.int32)
    grand = parent[parent]
    ancestor = ((nodes[None, :] == parent[:, None]) | (nodes[None, :] == grand[:, None])) & (
        nodes[None, :] != nodes[:, None]
    )
    node_hot = (node[:, None] == nodes[None, :]).astype(jnp.float32)
    perm_hot = (logical[:, None] == ar[None, :]).astype(jnp.float32)
    listed_store = jnp.dot(structure.astype(jnp.float32), perm_hot.T, precision=HIGHEST)
    anc_pairs = jnp.dot(
        node_hot, jnp.dot(ancestor.astype(jnp.float32), node_hot.T, precision=HIGHEST), precision=HIGHEST
    )
    list_pairs = jnp.dot(node_hot, listed_store, precision=HIGHEST)
    link = (anc_pairs * list_pairs).T > 0.5
    same = node[:, None] == node[None, :]
    return level, same, link


def masked(block_rows, mask):
    rblocks, width = mask.shape
    bsz = block_rows.shape[0] // rblocks
    shaped = block_rows.reshape(rblocks, bsz, width, bsz) * mask[:, None, :, None].astype(jnp.float32)
    return shaped.reshape(block_rows.shape)


def general_body(factor, rhs, parent, bounds, slot, structure, n_row):
    level, same, link = block_masks(parent, bounds, slot, structure)
    held = slot.shape[0] // n_row
    bsz = factor.shape[0] // held
    first = lax.axis_index("row") * held
    level_mine = lax.dynamic_slice_in_dim(level, first, held, 0)
    same_mine = lax.dynamic_slice_in_dim(same, first, held, 0)
    link_mine = lax.dynamic_slice_in_dim(link, first, held, 0)
    full_rows = lax.all_gather(factor, "col", axis=1, tiled=True)
    diag_part = masked(full_rows, same_mine)
    link_part = masked(full_rows, link_mine)

    def product(matrix, vector):
        return jnp.dot(
            matrix,
            lax.all_gather(vector, "row", axis=0, tiled=True),
            precision=HIGHEST,
            preferred_element_type=jnp.float32,
        )

    acc = jnp.zeros(rhs.shape, jnp.float32)
    result = jnp.zeros(rhs.shape, jnp.float32)
    for section in range(3):
        rows = jnp.repeat(level_mine == section, bsz)[:, None]
        solved = jnp.where(rows, product(diag_part, rhs - acc), 0.0)
        result = result + solved
        if section < 2:
            acc = acc + product(link_part, solved)
    return result


ON = 0
SAME = 3
PARTNER = 8
HEAD = 16
LINK0 = 0
LINK1 = 8
FACTS = 40

MASK_PAIRS = list(itertools.combinations(range(1, 8), 2))
MASK_SETS = [
    s for size in (3, 4) for s in itertools.combinations(range(1, 8), size) if functools.reduce(operator.xor, s) == 0
]


def mask_table():
    table = np.zeros(256, np.int32)
    for i, masks in enumerate(MASK_PAIRS + MASK_SETS):
        table[sum(1 << k for k in masks)] = i
    return table


def as_int(flag):
    return jnp.where(flag, jnp.int32(1), jnp.int32(0))


def fetch(pairs, sems):
    copies = [pltpu.make_async_copy(a, b, sems.at[i]) for i, (a, b) in enumerate(pairs)]
    for copy in copies:
        copy.start()
    for copy in copies:
        copy.wait()


def wide_block(bounds):
    wide = jnp.int32(0)
    for s in range(1, 7):
        wide = wide + as_int(bounds[s] == s)
    return wide


def level_of(node):
    return as_int(node >= 4) + as_int(node >= 6)


def set_row(masks, row, flag):
    masks[row : row + 1, :] = jnp.full((1, masks.shape[1]), as_int(flag).astype(F32))


def split_piece(j, piece, high, low):
    bsz = piece.shape[0]
    for h in range(2):
        high[2 * j + h], low[2 * j + h] = split(piece[:, h * bsz : (h + 1) * bsz])


def head_kernel(both, first, masks):
    bounds = [both[i : i + 1, :] for i in range(8)]
    slot = [both[8 + i : 9 + i, :] for i in range(8)]
    p = lax.axis_index("row")
    zero = jnp.zeros_like(bounds[0])
    wide = zero
    for s in range(1, 7):
        wide = wide + as_int(bounds[s] == s)
    m = zero
    place = zero
    for i in range(7):
        m = m + jnp.where(wide == i, slot[i] ^ slot[i + 1], 0)
        place = place + (i + 1) * as_int(slot[i + 1] == p)
    first[...] = jnp.where(wide < 4, m, 0)
    node = place - as_int(place > wide)
    partner = m ^ place_of(0)
    masks[...] = jnp.zeros(masks.shape, F32)
    for k in range(3):
        masks[ON + k : ON + k + 1, :] = as_int(level_of(node) == k).astype(F32)
    masks[SAME : SAME + 1, :] = as_int(node == wide).astype(F32)
    for k in range(8):
        masks[PARTNER + k : PARTNER + k + 1, :] = as_int((node == wide) & (partner == k)).astype(F32)


def facts_kernel(after, parent_in, bounds_in, slot_in, structure_in, table_in, masks, middle, spread, end, parent, bounds, slot, structure, table, logical, node, link1, sems):
    del after
    pairs = [(parent_in, parent), (bounds_in, bounds), (slot_in, slot), (structure_in, structure), (table_in, table)]
    fetch(pairs, sems)
    p = lax.axis_index("row")
    c = lax.axis_index("col")
    wide = wide_block(bounds)
    wide_level = level_of(wide)
    m = slot[wide] ^ slot[wide + 1]
    for i in range(8):
        q = slot[i]
        logical[q] = i
        node[q] = i - as_int(i > wide)
    mine = node[p]
    place = logical[p]

    def linked(q):
        below = node[q]
        up = parent[below]
        top = parent[up]
        above = ((mine == up) | (mine == top)) & (mine != below)
        return above & (structure[below, place] == 1)

    masks[...] = jnp.zeros(masks.shape, F32)
    for k in range(8):
        q = k ^ (2 * c)
        on = linked(q)
        set_row(masks, LINK0 + k, on & (node[q] < 4))
        link1[k] = as_int(on & (node[q] >= 4) & (node[q] < 6))
    at_one = wide_level == 1
    at_two = wide_level == 2
    top = slot[7]
    u = slot[jnp.where(at_two, 4, 5)] ^ top
    v = slot[jnp.where(at_two, 5, 6)] ^ top
    third = slot[4] ^ top
    fourth = u ^ v ^ third
    one = jnp.int32(1)
    bits = (one << u) | (one << v)
    bits = bits | jnp.where(at_one, (one << third) | ((one << fourth) & 254), 0)
    bits = bits | jnp.where(at_two, (one << (u ^ m)) | (one << (v ^ m)), 0)

    def set_index(index, value):
        index[...] = jnp.full(index.shape, value)

    set_index(middle, jnp.where(at_one, m, jnp.where(at_two, 8, 0)))
    set_index(spread, table[bits])
    set_index(end, jnp.where(at_one, 1, jnp.where(at_two, 1 + m, 0)))

    def set_link(s, mask, on):
        at = place_of(mask)

        @pl.when(on)
        def _():
            row = LINK1 + 8 * s + at
            masks[pl.ds(row, 1), :] = jnp.full((1, masks.shape[1]), link1[at].astype(F32))

    count = jnp.int32(0)
    for k in range(1, 8):
        on = (bits >> k) & 1
        set_link(count, k, on == 1)
        count = count + on


def split(value):
    high = value.astype(BF16)
    return high, (value - high.astype(F32)).astype(BF16)


def dot(high, low, value):
    value_high, value_low = split(value)
    small = jnp.dot(high, value_low, preferred_element_type=F32) + jnp.dot(low, value_high, preferred_element_type=F32)
    return jnp.dot(high, value_high, preferred_element_type=F32) + small


def dot_pair(high, low, places, blocks):
    both = [jnp.concatenate([part[places[0]], part[places[1]]], axis=1) for part in (high, low)]
    return dot(both[0], both[1], jnp.concatenate(blocks, axis=0))


def place_of(mask):
    return lax.axis_index("row") ^ mask ^ (2 * lax.axis_index("col"))


def row_of(masks, row):
    return masks[row : row + 1, :]


def own_part(head, high, low, level, mine):
    at = place_of(0)
    return dot(high[at], low[at], mine) * row_of(head, ON + level)


def partner_part(head, high, low, level, partner):
    on = row_of(head, SAME) * row_of(head, ON + level)
    block = [jnp.zeros(high.shape[1:], BF16) for _ in range(2)]
    for k in range(8):
        pick = row_of(head, PARTNER + k).astype(BF16)
        block = [block[0] + high[k] * pick, block[1] + low[k] * pick]
    return dot(block[0], block[1], jnp.where(on > 0, partner, 0.0))


def split_kernel(f1, f2, high, low):
    split_piece(1, f1, high, low)
    split_piece(2, f2, high, low)


def first_kernel(head, rhs, partner, f0, f3, high_in, low_in, y, high, low):
    del high_in, low_in
    split_piece(0, f0, high, low)
    split_piece(3, f3, high, low)
    y[...] = own_part(head, high, low, 0, rhs[...]) + partner_part(head, high, low, 0, partner[...])


def unread_kernel(*outs):
    del outs


def second_kernel(head, facts, rhs, high, low, *rest):
    ys, (t, y) = rest[:-2], rest[-2:]
    total = rhs[...]
    for k in range(0, 8, 2):
        places = [place_of(k), place_of(k + 1)]
        blocks = [ys[k + i][...] * facts[pl.ds(LINK0 + places[i], 1), :] for i in range(2)]
        total = total - dot_pair(high, low, places, blocks)
    t[...] = total
    y[...] = own_part(head, high, low, 1, total)


def partner_kernel(head, high, low, y_in, partner, y):
    y[...] = y_in[...] + partner_part(head, high, low, 1, partner[...])


def keep_kernel(*refs):
    half = len(refs) // 2
    for given, kept in zip(refs[:half], refs[half:]):
        kept[...] = given[...]


def less_linked(facts, high, low, t, zs):
    total = t
    for k in range(0, 8, 2):
        blocks = []
        for i in range(2):
            value = jnp.zeros(t.shape, F32)
            for s, z in enumerate(zs):
                value = value + jnp.where(row_of(facts, LINK1 + 8 * s + k + i) > 0, z, 0.0)
            blocks.append(value)
        total = total - dot_pair(high, low, [k, k + 1], blocks)
    return total


def residual_kernel(facts, high, low, t, z0, z1, z2, z3, total):
    total[...] = less_linked(facts, high, low, t[...], [z0[...], z1[...], z2[...], z3[...]])


def last_kernel(head, high, low, y0, y1, total, partner, out):
    y2 = own_part(head, high, low, 2, total[...]) + partner_part(head, high, low, 2, partner[...])
    out[...] = y0[...] + y1[...] + y2


def third_kernel(head, facts, high, low, t, y0, y1, *rest):
    zs, out = rest[:-1], rest[-1]
    total = less_linked(facts, high, low, t[...], [z[...] for z in zs])
    out[...] = y0[...] + y1[...] + own_part(head, high, low, 2, total)


def call(kernel, args, outs, aliases=()):
    outs = [jax.ShapeDtypeStruct(*o) if isinstance(o[0], tuple) else jax.ShapeDtypeStruct(o, F32) for o in outs]
    return pl.pallas_call(
        kernel,
        in_specs=[VMEM] * len(args),
        out_specs=[VMEM] * len(outs),
        out_shape=outs,
        input_output_aliases=dict(aliases),
        compiler_params=SMALL,
    )(*args)


def keep(blocks):
    return call(keep_kernel, blocks, [b.shape for b in blocks])


def unread(shape, count):
    if not count:
        return ()
    outs = [jax.ShapeDtypeStruct(shape, F32)] * count
    return pl.pallas_call(unread_kernel, out_specs=[ANY] * count, out_shape=outs, compiler_params=SMALL)()


def find_facts(after, parent, bounds, slot, structure, table):
    i32 = jnp.int32
    args = [parent, bounds, slot, structure, jnp.asarray(table)]
    index = jax.ShapeDtypeStruct((128,), i32)
    return pl.pallas_call(
        facts_kernel,
        in_specs=[ANY] * 6,
        out_specs=[VMEM] * 4,
        out_shape=[jax.ShapeDtypeStruct((FACTS, 128), F32), index, index, index],
        scratch_shapes=[pltpu.SMEM(a.shape, i32) for a in args]
        + [pltpu.SMEM((8,), i32)] * 3
        + [pltpu.SemaphoreType.DMA((5,))],
        compiler_params=SMALL,
    )(after, *args)


def find_head(bounds, slot):
    outs = [jax.ShapeDtypeStruct((1, 128), jnp.int32), jax.ShapeDtypeStruct((HEAD, 128), F32)]
    both = jnp.broadcast_to(jnp.concatenate([bounds, slot])[:, None], (16, 128))
    return pl.pallas_call(
        head_kernel, in_specs=[VMEM], out_specs=[VMEM] * 2, out_shape=outs, compiler_params=SMALL
    )(both)


def wide_body(factor, rhs, parent, bounds, slot, structure, n_row, n_col):
    bsz, cols = rhs.shape
    block = (bsz, cols)

    def send(value, row_mask, col_mask=0):
        pairs = [
            (r * n_col + k, (r ^ row_mask) * n_col + (k ^ col_mask)) for r in range(n_row) for k in range(n_col)
        ]
        return lax.ppermute(value, ("row", "col"), pairs)

    f0 = factor
    f2 = send(f0, 0, 2)
    first, head = find_head(bounds, slot)
    f1 = send(f0, 0, 1)

    def exchange(mask, value):
        return keep([send(value, mask)])[0] if mask else unread(block, 1)[0]

    partner = lax.switch(first[0, 0], [functools.partial(exchange, k) for k in range(n_row)], rhs)
    f2, partner = lax.optimization_barrier((f2, partner))
    f3 = send(f2, 0, 1)
    parts = ((n_row, bsz, bsz), BF16)
    high, low = call(split_kernel, [f1, f2], [parts, parts])
    y0, high, low = call(
        first_kernel, [head, rhs, partner, f0, f3, high, low], [block, parts, parts], {5: 1, 6: 2}
    )

    far = send(y0, 4)
    near = [send(y0, k) for k in (1, 2, 3)]
    ys = [y0] + near + [far] + [send(far, k) for k in (1, 2, 3)]
    facts, at_middle, at_spread, at_end = find_facts(near[0], parent, bounds, slot, structure, mask_table())
    t, y1 = call(second_kernel, [head, facts, rhs, high, low] + ys, [block, block])

    def middle(mask, head, high, low, t, y1):
        if not mask:
            return unread(block, 1)[0]
        if mask == n_row:
            return keep([y1])[0]
        return call(partner_kernel, [head, high, low, y1, send(t, mask)], [block])[0]

    fixed = lax.switch(
        at_middle[0], [functools.partial(middle, k) for k in range(n_row + 1)], head, high, low, t, y1
    )

    def spread(masks, y, fixed):
        blocks = keep([send(y if masks in MASK_PAIRS else fixed, k) for k in masks])
        return tuple([*blocks, *unread(block, 4 - len(masks))])

    zs = lax.switch(at_spread[0], [functools.partial(spread, masks) for masks in MASK_PAIRS + MASK_SETS], y1, fixed)
    def end(mask, head, facts, high, low, t, y0, y1, fixed, *zs):
        if mask == 0:
            return call(third_kernel, [head, facts, high, low, t, y0, y1, *zs[:2]], [block])[0]
        if mask is None:
            return call(third_kernel, [head, facts, high, low, t, y0, fixed, *zs], [block])[0]
        (total,) = call(residual_kernel, [facts, high, low, t, *zs], [block])
        return call(last_kernel, [head, high, low, y0, y1, total, send(total, mask)], [block])[0]

    return lax.switch(
        at_end[0],
        [functools.partial(end, k) for k in [0, None] + list(range(1, n_row))],
        *(head, facts, high, low, t, y0, y1, fixed, *zs),
    )


def body(factor, rhs, parent, bounds, slot, structure, n_row, n_col):
    count = slot.shape[0]
    if count == 8 and n_row == 8 and n_col == 4 and bounds.shape[0] == 8:
        return wide_body(factor, rhs, parent, bounds, slot, structure, n_row, n_col)
    return general_body(factor, rhs, parent, bounds, slot, structure, n_row)


def solution(mesh):
    in_specs = (P("row", "col"), P("row", "col"), P(), P(), P(), P())
    out_specs = P("row", "col")
    step = functools.partial(body, n_row=mesh.shape["row"], n_col=mesh.shape["col"])
    return jax.shard_map(step, mesh=mesh, in_specs=in_specs, out_specs=out_specs, check_vma=False)
```
